32 devices in a mesh: row: 4 (over y, x), col: 8 (over z, core).
Axes of the slice: x: 2, y: 2, z: 4, core: 2. Of those that a mesh axis runs over, the one named last changes fastest.
Arguments:
- inputs: bfloat16 [128, 448, 128], P('row', 'col'), may hold values from -6 to 6
- cotangent: bfloat16 [128, 448, 128], P('row', 'col'), may hold values from -6 to 6
- w_conv: bfloat16 [3, 3, 128, 128], replicated, may hold values from -0.1875 to 0.1875
- w_down: bfloat16 [3, 3, 128, 256], replicated, may hold values from -0.1875 to 0.1875
- w_up: bfloat16 [2, 2, 256, 128], replicated, may hold values from -0.375 to 0.375
Outputs:
- output: bfloat16 [128, 448, 128], P('row', 'col')
- grad_inputs: bfloat16 [128, 448, 128], P('row', 'col')
- grad_conv: float32 [147456], P(('row', 'col'))
- grad_down: float32 [294912], P(('row', 'col'))
- grad_up: float32 [131072], P(('row', 'col'))
The draws below stay inside these ranges and needn't reach their ends.
All inputs are finite; a program needn't handle non-finite values.
Results may differ from the reference program's by a relative error of at most 0.013.
Values may be sent and summed in bfloat16 or wider, within the bound.
A program may use at most 64 MiB of HBM per device.

```python
import jax
import jax.numpy as jnp
from jax import lax

C1 = 128
C2 = 256
NH = 128
NW = 448


def block_levels(own_key, shape, shards, least, largest):
    level = 1.0
    for axis_at, shards_of in shards:
        heights = jax.random.uniform(jax.random.fold_in(jax.random.fold_in(own_key, 6), axis_at), (shards_of,), jnp.float32, least / len(shards), largest / len(shards))
        level = level * jnp.repeat(jnp.exp(heights), shape[axis_at] // shards_of).reshape((-1,) + (1,) * (len(shape) - 1 - axis_at))
    return level


def noise(stream_key, dims, spread, most, split=(), held_as=jnp.bfloat16):
    drawn = jax.random.normal(stream_key, dims, jnp.float32) * spread
    if len(split) > 0:
        drawn = block_levels(stream_key, dims, split, -0.22, 0.18) * drawn
    return jnp.clip(drawn, min=-most, max=most).astype(held_as)


def setup_inputs(seed: int = 0) -> dict:
    key_list = jax.random.split(jax.random.key(seed), 6)
    return {
        "inputs": noise(key_list[0], (NH, NW, C1), 1.0, 6.0, ((0, 4), (1, 8))),
        "cotangent": noise(key_list[1], (NH, NW, C1), 1.0, 6.0, ((0, 4), (1, 8))),
        "w_conv": noise(key_list[2], (3, 3, C1, C1), (9 * C1) ** -0.5, 0.1875),
        "w_down": noise(key_list[3], (3, 3, C1, C2), (9 * C1) ** -0.5, 0.1875),
        "w_up": noise(key_list[4], (2, 2, C2, C1), C2 ** -0.5, 0.375),
    }


def conv_same(field, kernel):
    return lax.conv_general_dilated(field[None], kernel, (1, 1), ((1, 1), (1, 1)), dimension_numbers=('NHWC', 'HWIO', 'NHWC'), precision=lax.Precision.HIGHEST)[0]

def conv_down(field, kernel):
    return lax.conv_general_dilated(field[None], kernel, (2, 2), ((1, 1), (1, 1)), dimension_numbers=('NHWC', 'HWIO', 'NHWC'), precision=lax.Precision.HIGHEST)[0]

def silu_slope(value):
    sig = jax.nn.sigmoid(value)
    return sig * (1.0 + value * (1.0 - sig))

def forward_fine(inputs, w_conv):
    pre = conv_same(inputs.astype(jnp.float32), w_conv.astype(jnp.float32))
    return (pre, jax.nn.silu(pre).astype(jnp.bfloat16))

def reference(inputs, cotangent, w_conv, w_down, w_up):
    pre, fine = forward_fine(inputs, w_conv)
    coarse_pre = conv_down(fine.astype(jnp.float32), w_down.astype(jnp.float32))
    coarse = jax.nn.silu(coarse_pre).astype(jnp.bfloat16)
    up_f = w_up.astype(jnp.float32)
    upsampled = jnp.einsum('mnc,pqco->mpnqo', coarse.astype(jnp.float32), up_f, precision=lax.Precision.HIGHEST).reshape(NH, NW, C1)
    output = (fine.astype(jnp.float32) + upsampled).astype(jnp.bfloat16)
    upsampled = None
    cot_r = cotangent.astype(jnp.float32).reshape(NH // 2, 2, NW // 2, 2, C1)
    grad_coarse = jnp.einsum('mpnqo,pqco->mnc', cot_r, up_f, precision=lax.Precision.HIGHEST)
    up_sum = jnp.einsum('mnc,mpnqo->pqco', coarse.astype(jnp.float32), cot_r, precision=lax.Precision.HIGHEST)
    cot_r = None
    grad_cpre = (grad_coarse * silu_slope(coarse_pre)).astype(jnp.bfloat16)
    _, back_down = jax.vjp(conv_down, fine.astype(jnp.float32), w_down.astype(jnp.float32))
    down_in, down_sum = back_down(grad_cpre.astype(jnp.float32))
    grad_fine = cotangent.astype(jnp.float32) + down_in
    down_in = None
    grad_pre = (grad_fine * silu_slope(pre)).astype(jnp.bfloat16)
    grad_fine = None
    pre = None
    _, back_conv = jax.vjp(conv_same, inputs.astype(jnp.float32), w_conv.astype(jnp.float32))
    grad_x, conv_sum = back_conv(grad_pre.astype(jnp.float32))
    grad_inputs = grad_x.astype(jnp.bfloat16)
    scale = 1.0 / jnp.sqrt(jnp.float32(NH * NW))
    return (output, grad_inputs, (conv_sum * scale).reshape(-1), (down_sum * scale).reshape(-1), (up_sum * scale).reshape(-1))
```

```python
import functools
import math

import jax
import jax.numpy as jnp
from jax import lax
from jax.experimental import pallas as pl
from jax.experimental.pallas import tpu as pltpu
from jax.sharding import PartitionSpec as P

MESH = pl.DeviceIdType.MESH
F32 = jnp.float32
BF16 = jnp.bfloat16
VMEM = pl.BlockSpec(memory_space=pltpu.VMEM)
NT = (((1,), (1,)), ((), ()))
TN = (((0,), (0,)), ((), ()))
SHIFTS = [(dr, dc) for dr in (-1, 0, 1) for dc in (-1, 0, 1) if (dr, dc) != (0, 0)]


def dot(a, b):
    return jnp.dot(a, b, preferred_element_type=F32)


def dot_nt(a, b):
    return lax.dot_general(a, b, NT, preferred_element_type=F32)


def dot_tn(a, b):
    return lax.dot_general(a, b, TN, preferred_element_type=F32)


def halo_kernel(n_row, n_col, x_ref, ct_ref, *rest):
    outs, (pack, send_sem, recv_sem) = rest[:10], rest[10:]
    x_top, x_bot, ct_top, ct_bot, left, right, tl, tr, bl, br = outs
    rows, cols, _ = x_ref.shape
    r, c = lax.axis_index("row"), lax.axis_index("col")

    def exists(dr, dc):
        ok = None
        for d, at, n in ((dr, r, n_row), (dc, c, n_col)):
            if d:
                here = at > 0 if d < 0 else at < n - 1
                ok = here if ok is None else jnp.logical_and(ok, here)
        return ok

    barrier = pltpu.get_barrier_semaphore()
    for dr, dc in SHIFTS:

        @pl.when(exists(dr, dc))
        def _(dr=dr, dc=dc):
            pl.semaphore_signal(barrier, inc=1, device_id=(r + dr, c + dc), device_id_type=MESH)

    pack[0] = jnp.concatenate(
        [x_ref[:, 0:8, :].astype(F32), ct_ref[:, 0:8, :].astype(F32)], axis=1
    ).astype(BF16)
    pack[1] = jnp.concatenate(
        [x_ref[:, cols - 8 : cols, :].astype(F32), ct_ref[:, cols - 8 : cols, :].astype(F32)],
        axis=1,
    ).astype(BF16)
    near_r = 3 - (r == 0).astype(jnp.int32) - (r == n_row - 1).astype(jnp.int32)
    near_c = 3 - (c == 0).astype(jnp.int32) - (c == n_col - 1).astype(jnp.int32)
    pl.semaphore_wait(barrier, near_r * near_c - 1)

    low, high = pl.ds(0, 4), pl.ds(rows - 4, 4)
    plan = [
        ((1, 0), x_ref.at[high], x_top),
        ((-1, 0), x_ref.at[low], x_bot),
        ((1, 0), ct_ref.at[high], ct_top),
        ((-1, 0), ct_ref.at[low], ct_bot),
        ((0, 1), pack.at[1], left),
        ((0, -1), pack.at[0], right),
        ((1, 1), pack.at[1, high], tl),
        ((1, -1), pack.at[0, high], tr),
        ((-1, 1), pack.at[1, low], bl),
        ((-1, -1), pack.at[0, low], br),
    ]

    def copy(k):
        (dr, dc), src, dst = plan[k]
        return pltpu.make_async_remote_copy(
            src_ref=src,
            dst_ref=dst,
            send_sem=send_sem.at[k],
            recv_sem=recv_sem.at[k],
            device_id=(r + dr, c + dc),
            device_id_type=MESH,
        )

    for k, ((dr, dc), _, _) in enumerate(plan):

        @pl.when(exists(dr, dc))
        def _(k=k):
            copy(k).start()

    for k, ((dr, dc), _, _) in enumerate(plan):

        @pl.when(exists(dr, dc))
        def _(k=k):
            copy(k).wait_send()

        @pl.when(exists(-dr, -dc))
        def _(k=k):
            copy(k).wait_recv()


def halos(n_row, n_col, x, ct):
    rows, cols, width = x.shape
    shapes = [(4, cols, width)] * 4 + [(rows, 16, width)] * 2 + [(4, 16, width)] * 4
    return pl.pallas_call(
        functools.partial(halo_kernel, n_row, n_col),
        out_shape=[jax.ShapeDtypeStruct(s, BF16) for s in shapes],
        in_specs=[VMEM] * 2,
        out_specs=[VMEM] * 10,
        scratch_shapes=[
            pltpu.VMEM((2, rows, 16, width), BF16),
            pltpu.SemaphoreType.DMA((10,)),
            pltpu.SemaphoreType.DMA((10,)),
        ],
        compiler_params=pltpu.CompilerParams(
            collective_id=0, has_side_effects=True, vmem_limit_bytes=32 * 2**20
        ),
        name="halos",
    )(x, ct)


def level_kernel(n_row, n_col, *refs):
    (x_ref, ct_ref, x_top, x_bot, ct_top, ct_bot, left, right, tl, tr, bl, br, wc, wd, wu) = refs[:15]
    (out_ref, gx_ref, conv_sum, down_sum, up_sum) = refs[15:20]
    (xf, x3, ce, fine, slope, d3, t4, cp, co, g, gp, g3, up) = refs[20:]
    rows, cols, ch = x_ref.shape
    wide = wd.shape[3]
    r, c = lax.axis_index("row"), lax.axis_index("col")
    has_top, has_bot = r > 0, r < n_row - 1
    has_left, has_right = c > 0, c < n_col - 1
    ce_rows, a_rows, u_rows = rows + 4, rows + 6, rows // 2 + 2
    half = rows // 2

    def assemble(dst, offset, at, own, lft, rgt, row_ok):
        n = own.shape[0]
        ok_l, ok_r = has_left, has_right
        if row_ok is not None:
            own = jnp.where(row_ok, own.astype(F32), 0.0)
            ok_l = jnp.logical_and(ok_l, row_ok)
            ok_r = jnp.logical_and(ok_r, row_ok)
        rows_at = pl.ds(at, n)
        dst[rows_at, 0:offset, :] = jnp.where(ok_l, lft.astype(F32), 0.0)[:, 8 - offset : 8, :]
        dst[rows_at, offset : offset + cols, :] = own.astype(F32)
        dst[rows_at, offset + cols : offset + cols + 8, :] = jnp.where(ok_r, rgt.astype(F32), 0.0)

    xs, cs = slice(0, 8), slice(8, 16)
    xf[:, 64:72, :] = jnp.zeros((rows + 8, 8, ch), F32)
    ce[:, 64:72, :] = jnp.zeros((ce_rows, 8, ch), F32)
    assemble(xf, 4, 0, x_top[...], tl[:, xs, :], tr[:, xs, :], has_top)
    assemble(xf, 4, rows + 4, x_bot[...], bl[:, xs, :], br[:, xs, :], has_bot)
    assemble(ce, 3, 0, ct_top[2:4], tl[2:4, cs, :], tr[2:4, cs, :], has_top)
    assemble(ce, 3, rows + 2, ct_bot[0:2], bl[0:2, cs, :], br[0:2, cs, :], has_bot)

    @pl.loop(0, rows // 8)
    def _(k):
        at = pl.ds(k * 8, 8)
        assemble(xf, 4, 4 + k * 8, x_ref[at], left[at, xs, :], right[at, xs, :], None)
        assemble(ce, 3, 2 + k * 8, ct_ref[at], left[at, cs, :], right[at, cs, :], None)

    @pl.loop(0, (rows + 8) // 4)
    def _(k):
        at = pl.ds(k * 4, 4)
        for q in range(3):
            x3[at, :, q * ch : (q + 1) * ch] = xf[at, q : q + 64, :].astype(BF16)

    wc_rows = wc[...].reshape(3, 3 * ch, ch)
    j_at = lax.broadcasted_iota(jnp.int32, (1, 64, 1), 1) - 3
    col_ok = jnp.logical_and(
        jnp.logical_or(j_at >= 0, has_left), jnp.logical_or(j_at < cols, has_right)
    )
    fine[:, 64:72, :] = jnp.zeros((a_rows, 8, ch), F32)
    slope[:, 64:72, :] = jnp.zeros((a_rows, 8, ch), F32)
    gp[:, 64:72, :] = jnp.zeros((a_rows, 8, ch), F32)

    def in_grid(first, n):
        i_at = lax.broadcasted_iota(jnp.int32, (n, 1, 1), 0) + (first - 3)
        row_ok = jnp.logical_and(
            jnp.logical_or(i_at >= 0, has_top), jnp.logical_or(i_at < rows, has_bot)
        )
        return jnp.logical_and(row_ok, col_ok)

    step = a_rows // 2

    @pl.loop(0, 2)
    def _(k):
        pre = None
        for p in range(3):
            term = dot(x3[pl.ds(k * step + p, step)].reshape(step * 64, 3 * ch), wc_rows[p])
            pre = term if pre is None else pre + term
        sig = jax.nn.sigmoid(pre)
        at = pl.ds(k * step, step)
        ok = in_grid(k * step, step)
        value = (pre * sig).reshape(step, 64, ch)
        fine[at, 0:64, :] = jnp.where(ok, value, 0.0)
        slope[at, 0:64, :] = (sig * (1.0 + pre * (1.0 - sig))).reshape(step, 64, ch)

    @pl.loop(0, a_rows // 2)
    def _(k):
        for p in range(2):
            for q in range(3):
                d3[k, p, :, q * ch : (q + 1) * ch] = fine[
                    2 * k + p, pl.ds(q, 32, stride=2), :
                ].astype(BF16)

    @pl.loop(0, u_rows)
    def _(k):
        for p in range(2):
            for q in range(2):
                e = 2 * p + q
                t4[k, :, e * ch : (e + 1) * ch] = ce[
                    2 * k + p, pl.ds(1 + q, 32, stride=2), :
                ].astype(BF16)

    wd_rows = wd[...].reshape(3, 3 * ch, wide)
    cpre = None
    for p in range(3):
        window = d3[p // 2 : p // 2 + u_rows, p % 2].reshape(u_rows * 32, 3 * ch)
        term = dot(window, wd_rows[p])
        cpre = term if cpre is None else cpre + term
    cp[...] = cpre.reshape(u_rows, 32, wide)
    v_at = lax.broadcasted_iota(jnp.int32, (1, 32, 1), 1) - 1
    v_own = jnp.logical_and(v_at >= 0, v_at < cols // 2)
    sig = jax.nn.sigmoid(cp[...])
    co[...] = (cp[...] * sig).astype(BF16)
    grad = None
    for e in range(4):
        term = dot_nt(
            t4[:, :, e * ch : (e + 1) * ch].reshape(u_rows * 32, ch), wu[e // 2, e % 2]
        )
        grad = term if grad is None else grad + term
    u_at = lax.broadcasted_iota(jnp.int32, (u_rows, 1, 1), 0) - 1
    ok = jnp.logical_and(
        jnp.logical_and(jnp.logical_or(u_at >= 0, has_top), jnp.logical_or(u_at < half, has_bot)),
        jnp.logical_and(
            jnp.logical_or(v_at >= 0, has_left), jnp.logical_or(v_at < cols // 2, has_right)
        ),
    )
    full = cp[...]
    sig = jax.nn.sigmoid(full)
    part = grad.reshape(u_rows, 32, wide) * (sig * (1.0 + full * (1.0 - sig)))
    g[:, 32:40, :] = jnp.zeros((u_rows, 8, wide), F32)
    g[:, 0:32, :] = jnp.where(ok, part, 0.0)

    co_rows = co[1 : half + 1].reshape(half * 32, wide)
    for e in range(4):
        p, q = e // 2, e % 2
        res = dot(co_rows, wu[p, q]).reshape(half, 32, ch)
        for m in range(half):
            up[2 * m + p, pl.ds(1 + q, 32, stride=2), :] = res[m]

    @pl.loop(0, rows // 4)
    def _(k):
        f = fine[pl.ds(3 + k * 4, 4), 3 : 3 + cols, :].astype(BF16).astype(F32)
        out_ref[pl.ds(k * 4, 4)] = (f + up[pl.ds(k * 4, 4), 3 : 3 + cols, :]).astype(BF16)

    own_co = jnp.where(v_own, co[1 : half + 1].astype(F32), 0.0).astype(BF16)
    us = dot_tn(own_co.reshape(half * 32, wide), t4[1 : half + 1].reshape(half * 32, 4 * ch))
    for e in range(4):
        up_sum[e * wide : (e + 1) * wide, :] = us[:, e * ch : (e + 1) * ch]
    own_g = jnp.where(v_own, g[1 : half + 1, 0:32, :], 0.0).astype(BF16).reshape(half * 32, wide)
    for p in range(3):
        window = d3[p // 2 + 1 : p // 2 + 1 + half, p % 2].reshape(half * 32, 3 * ch)
        down_sum[p * 3 * ch : (p + 1) * 3 * ch, :] = dot_tn(window, own_g)

    g_here = g[:, 0:32, :].astype(BF16).reshape(u_rows * 32, wide)
    g_next = g[:, 1:33, :].astype(BF16).reshape(u_rows * 32, wide)
    less = (u_rows - 1) * 32

    def pair(p):
        return jnp.concatenate([wd[p, 1], wd[p, 2]], axis=0)

    even = dot_nt(g_here, pair(1))
    even_odd = even[:, ch:] + dot_nt(g_next, wd[1, 0])
    odd = dot_nt(g_here[32:], pair(0)) + dot_nt(g_here[:less], pair(2))
    odd_odd = odd[:, ch:] + dot_nt(g_next[32:], wd[0, 0]) + dot_nt(g_next[:less], wd[2, 0])
    spread = {
        (0, 0): even[:, :ch],
        (0, 1): even_odd,
        (1, 0): odd[:, :ch],
        (1, 1): odd_odd,
    }
    for (s, t), value in spread.items():
        for u in range(u_rows - s):
            at = pl.ds(1 + t, 32, stride=2)
            ce[2 * u + s, at, :] = ce[2 * u + s, at, :] + value[u * 32 : (u + 1) * 32]

    @pl.loop(0, (rows + 2) // 2)
    def _(k):
        a = 2 + 2 * k
        value = ce[pl.ds(a - 1, 2), 0:64, :] * slope[pl.ds(a, 2), 0:64, :]
        gp[pl.ds(a, 2), 0:64, :] = jnp.where(in_grid(a, 2), value, 0.0)

    @pl.loop(0, (rows + 2) // 2)
    def _(k):
        at = pl.ds(2 + 2 * k, 2)
        for q in range(3):
            g3[at, :, q * ch : (q + 1) * ch] = gp[at, 4 - q : 68 - q, :].astype(BF16)

    j_own = jnp.logical_and(j_at >= 0, j_at < cols)
    own = jnp.where(j_own, gp[3 : rows + 3, 0:64, :], 0.0).astype(BF16)

    def shift(p):
        pieces = [own]
        if p > 0:
            pieces.insert(0, jnp.zeros((p, 64, ch), BF16))
        if p < 2:
            pieces.append(jnp.zeros((2 - p, 64, ch), BF16))
        return jnp.concatenate(pieces, axis=0).reshape((rows + 2) * 64, ch)

    shifted = [shift(p) for p in range(3)]
    sums = dot_tn(
        x3[3 : rows + 5].reshape((rows + 2) * 64, 3 * ch), jnp.concatenate(shifted, axis=1)
    )
    for p in range(3):
        conv_sum[p * 3 * ch : (p + 1) * 3 * ch, :] = sums[:, p * ch : (p + 1) * ch]

    turned = [jnp.concatenate([wc[p, q] for q in range(3)], axis=1) for p in range(3)]
    part_rows = rows // 2

    @pl.loop(0, 2)
    def _(k):
        total = None
        for p in range(3):
            window = g3[pl.ds(k * part_rows + 4 - p, part_rows)].reshape(part_rows * 64, 3 * ch)
            term = dot_nt(window, turned[p])
            total = term if total is None else total + term
        total = total.reshape(part_rows, 64, ch)[:, :cols, :]
        gx_ref[pl.ds(k * part_rows, part_rows)] = total.astype(BF16)


def level(n_row, n_col, x, ct, edges, wc, wd, wu):
    rows, cols, ch = x.shape
    wide = wd.shape[3]
    a_rows, u_rows = rows + 6, rows // 2 + 2
    return pl.pallas_call(
        functools.partial(level_kernel, n_row, n_col),
        out_shape=[
            jax.ShapeDtypeStruct(x.shape, BF16),
            jax.ShapeDtypeStruct(x.shape, BF16),
            jax.ShapeDtypeStruct((9 * ch, ch), F32),
            jax.ShapeDtypeStruct((9 * ch, wide), F32),
            jax.ShapeDtypeStruct((4 * wide, ch), F32),
        ],
        in_specs=[VMEM] * 15,
        out_specs=[VMEM] * 5,
        scratch_shapes=[
            pltpu.VMEM((rows + 8, 72, ch), F32),
            pltpu.VMEM((rows + 8, 64, 3 * ch), BF16),
            pltpu.VMEM((rows + 4, 72, ch), F32),
            pltpu.VMEM((a_rows, 72, ch), F32),
            pltpu.VMEM((a_rows, 72, ch), F32),
            pltpu.VMEM((a_rows // 2, 2, 32, 3 * ch), BF16),
            pltpu.VMEM((u_rows, 32, 4 * ch), BF16),
            pltpu.VMEM((u_rows, 32, wide), F32),
            pltpu.VMEM((u_rows, 32, wide), BF16),
            pltpu.VMEM((u_rows, 40, wide), F32),
            pltpu.VMEM((a_rows, 72, ch), F32),
            pltpu.VMEM((a_rows, 64, 3 * ch), BF16),
            pltpu.VMEM((rows, 72, ch), F32),
        ],
        compiler_params=pltpu.CompilerParams(vmem_limit_bytes=56 * 2**20),
        name="level",
    )(x, ct, *edges, wc, wd, wu)


def sum_kernel(n_row, n_col, scale, conv, down, up, conv_out, down_out, up_out, *rest):
    stage, recv0, acc1, recv1, acc2, recv2, send_sem, recv_sem = rest
    nz = n_col // 2
    blocks = n_row * n_col
    nc, nd, nu = conv.shape[0] // blocks, down.shape[0] // blocks, up.shape[0] // blocks
    r, c = lax.axis_index("row"), lax.axis_index("col")
    z, core = c // 2, c % 2
    peers = [(r, z * 2 + 1 - core)]
    peers += [((r + k) % n_row, c) for k in range(1, n_row)]
    peers += [(r, ((z + k) % nz) * 2 + core) for k in range(1, nz)]
    barrier = pltpu.get_barrier_semaphore()
    for peer in peers:
        pl.semaphore_signal(barrier, inc=1, device_id=peer, device_id_type=MESH)
    pad = stage.shape[1] - nu - 2 * nd - nc
    for row in range(n_row):
        for col in range(n_col):
            d = row * n_col + col
            slot = (col % 2) * (n_row * nz) + row * nz + col // 2
            pieces = [
                up[d * nu : (d + 1) * nu, :],
                down[d * nd : (d + 1) * nd, 0:128],
                down[d * nd : (d + 1) * nd, 128:256],
                conv[d * nc : (d + 1) * nc, :],
                jnp.zeros((pad, 128), F32),
            ]
            stage[slot] = jnp.concatenate(pieces, axis=0).astype(BF16)
    pl.semaphore_wait(barrier, len(peers))

    def copy(k, src, dst):
        return pltpu.make_async_remote_copy(
            src_ref=src,
            dst_ref=dst,
            send_sem=send_sem.at[k],
            recv_sem=recv_sem.at[k],
            device_id=peers[k],
            device_id_type=MESH,
        )

    per_core = n_row * nz
    first = copy(0, stage.at[pl.ds((1 - core) * per_core, per_core)], recv0)
    first.start()
    first.wait()
    for k in range(per_core):
        own = stage[core * per_core + k].astype(F32)
        acc1[k // nz, k % nz] = (own + recv0[k].astype(F32)).astype(BF16)
    copies = [copy(k, acc1.at[(r + k) % n_row], recv1.at[k - 1]) for k in range(1, n_row)]
    for item in copies:
        item.start()
    for item in copies:
        item.wait()
    for k in range(nz):
        total = acc1[r, k].astype(F32)
        for m in range(n_row - 1):
            total = total + recv1[m, k].astype(F32)
        acc2[k] = total.astype(BF16)
    copies = [
        copy(n_row - 1 + k, acc2.at[(z + k) % nz], recv2.at[k - 1]) for k in range(1, nz)
    ]
    for item in copies:
        item.start()
    for item in copies:
        item.wait()
    total = acc2[z].astype(F32)
    for m in range(nz - 1):
        total = total + recv2[m].astype(F32)
    total = total * scale
    up_out[...] = total[0:nu]
    down_out[:, 0:128] = total[nu : nu + nd]
    down_out[:, 128:256] = total[nu + nd : nu + 2 * nd]
    conv_out[...] = total[nu + 2 * nd : nu + 2 * nd + nc]


def scattered(n_row, n_col, scale, conv, down, up):
    blocks, nz = n_row * n_col, n_col // 2
    sizes = [a.shape[0] // blocks for a in (conv, down, up)]
    height = -(-(sizes[0] + 2 * sizes[1] + sizes[2]) // 16) * 16
    return pl.pallas_call(
        functools.partial(sum_kernel, n_row, n_col, scale),
        out_shape=[
            jax.ShapeDtypeStruct((n, a.shape[1]), F32)
            for n, a in zip(sizes, (conv, down, up))
        ],
        in_specs=[VMEM] * 3,
        out_specs=[VMEM] * 3,
        scratch_shapes=[
            pltpu.VMEM((blocks, height, 128), BF16),
            pltpu.VMEM((n_row * nz, height, 128), BF16),
            pltpu.VMEM((n_row, nz, height, 128), BF16),
            pltpu.VMEM((n_row - 1, nz, height, 128), BF16),
            pltpu.VMEM((nz, height, 128), BF16),
            pltpu.VMEM((nz - 1, height, 128), BF16),
            pltpu.SemaphoreType.DMA((n_row + nz - 1,)),
            pltpu.SemaphoreType.DMA((n_row + nz - 1,)),
        ],
        compiler_params=pltpu.CompilerParams(
            collective_id=1, has_side_effects=True, vmem_limit_bytes=48 * 2**20
        ),
        name="sums",
    )(conv, down, up)


def body(n_row, n_col, inputs, cotangent, w_conv, w_down, w_up):
    rows, cols, _ = inputs.shape
    edges = halos(n_row, n_col, inputs, cotangent)
    output, grad_inputs, *sums = level(
        n_row, n_col, inputs, cotangent, edges, w_conv, w_down, w_up
    )
    scale = 1.0 / math.sqrt(rows * n_row * cols * n_col)
    blocks = n_row * n_col
    if all(a.shape[0] % blocks == 0 for a in sums):
        sums = scattered(n_row, n_col, scale, *sums)
        return (output, grad_inputs, *(a.reshape(-1) for a in sums))
    sums = [
        lax.psum_scatter(a.reshape(-1), ("row", "col"), scatter_dimension=0, tiled=True) * scale
        for a in sums
    ]
    return (output, grad_inputs, *sums)


def solution(mesh):
    return jax.shard_map(
        functools.partial(body, mesh.shape["row"], mesh.shape["col"]),
        mesh=mesh,
        in_specs=(P("row", "col", None), P("row", "col", None), P(), P(), P()),
        out_specs=(
            P("row", "col", None),
            P("row", "col", None),
            P(("row", "col")),
            P(("row", "col")),
            P(("row", "col")),
        ),
        check_vma=False,
    )
```

```python
import functools
import math

import jax
import jax.numpy as jnp
from jax import lax
from jax.experimental import pallas as pl
from jax.experimental.pallas import tpu as pltpu
from jax.sharding import PartitionSpec as P

MESH = pl.DeviceIdType.MESH
F32 = jnp.float32
BF16 = jnp.bfloat16
VMEM = pl.BlockSpec(memory_space=pltpu.VMEM)
NT = (((1,), (1,)), ((), ()))
TN = (((0,), (0,)), ((), ()))
SHIFTS = [(dr, dc) for dr in (-1, 0, 1) for dc in (-1, 0, 1) if (dr, dc) != (0, 0)]


def dot(a, b):
    return jnp.dot(a, b, preferred_element_type=F32)


def dot_nt(a, b):
    return lax.dot_general(a, b, NT, preferred_element_type=F32)


def dot_tn(a, b):
    return lax.dot_general(a, b, TN, preferred_element_type=F32)


def exists(at, n, d):
    return at > 0 if d < 0 else at < n - 1


def level_kernel(n_row, n_col, reduce, *refs):
    x_hbm, ct_hbm, wc_hbm, wd_hbm, wu_hbm, out_hbm, gx_hbm, conv_out, down_out, up_out = refs[:10]
    x_ref, ct_ref, wc, wd, wu, out_ref, gx_ref, pack = refs[10:18]
    x_top, x_bot, ct_top, ct_bot, left, right, tl, tr, bl, br = edges = refs[18:28]
    (xf, x3, ce, fine, slope, d3, t4, cp, co, g, gp, g3, up) = refs[28:41]
    send_sem, recv_sem, local_sem = refs[41:44]
    conv_sum, down_sum, up_sum = refs[44:47] if reduce else (conv_out, down_out, up_out)
    rows, cols, ch = x_ref.shape
    wide = wd.shape[3]
    nz = n_col // 2
    r, c = lax.axis_index("row"), lax.axis_index("col")
    z, core = c // 2, c % 2
    has_top, has_bot = r > 0, r < n_row - 1
    has_left, has_right = c > 0, c < n_col - 1
    ce_rows, a_rows, u_rows = rows + 4, rows + 6, rows // 2 + 2
    half = rows // 2

    loads = [
        pltpu.make_async_copy(src, dst, local_sem.at[k])
        for k, (src, dst) in enumerate(
            [(x_hbm, x_ref), (ct_hbm, ct_ref), (wc_hbm, wc), (wd_hbm, wd), (wu_hbm, wu)]
        )
    ]
    for item in loads:
        item.start()

    def near(dr, dc):
        ok = None
        for d, at, n in ((dr, r, n_row), (dc, c, n_col)):
            if d:
                here = exists(at, n, d)
                ok = here if ok is None else jnp.logical_and(ok, here)
        return ok

    peers = [(r, z * 2 + 1 - core)]
    peers += [((r + k) % n_row, c) for k in range(1, n_row)]
    peers += [(r, ((z + k) % nz) * 2 + core) for k in range(1, nz)]
    if not reduce:
        peers = []
    barrier = pltpu.get_barrier_semaphore()
    for dr, dc in SHIFTS:

        @pl.when(near(dr, dc))
        def _(dr=dr, dc=dc):
            pl.semaphore_signal(barrier, inc=1, device_id=(r + dr, c + dc), device_id_type=MESH)

    for peer in peers:
        pl.semaphore_signal(barrier, inc=1, device_id=peer, device_id_type=MESH)

    loads[0].wait()
    loads[1].wait()
    for side, at in ((0, 0), (1, cols - 8)):
        pack[side] = jnp.concatenate(
            [x_ref[:, at : at + 8, :].astype(F32), ct_ref[:, at : at + 8, :].astype(F32)], axis=1
        ).astype(BF16)
    near_r = 3 - (r == 0).astype(jnp.int32) - (r == n_row - 1).astype(jnp.int32)
    near_c = 3 - (c == 0).astype(jnp.int32) - (c == n_col - 1).astype(jnp.int32)
    pl.semaphore_wait(barrier, near_r * near_c - 1 + len(peers))

    low, high = pl.ds(0, 4), pl.ds(rows - 4, 4)
    plan = [
        ((1, 0), x_ref.at[high], x_top),
        ((-1, 0), x_ref.at[low], x_bot),
        ((1, 0), ct_ref.at[pl.ds(rows - 2, 2)], ct_top),
        ((-1, 0), ct_ref.at[pl.ds(0, 2)], ct_bot),
        ((0, 1), pack.at[1], left),
        ((0, -1), pack.at[0], right),
        ((1, 1), pack.at[1, high], tl),
        ((1, -1), pack.at[0, high], tr),
        ((-1, 1), pack.at[1, low], bl),
        ((-1, -1), pack.at[0, low], br),
    ]

    def remote(k, src, dst, device):
        return pltpu.make_async_remote_copy(
            src_ref=src,
            dst_ref=dst,
            send_sem=send_sem.at[k],
            recv_sem=recv_sem.at[k],
            device_id=device,
            device_id_type=MESH,
        )

    def edge(k):
        (dr, dc), src, dst = plan[k]
        return remote(k, src, dst, (r + dr, c + dc))

    for k, ((dr, dc), _, _) in enumerate(plan):

        @pl.when(near(dr, dc))
        def _(k=k):
            edge(k).start()

    xf[:, 64:72, :] = jnp.zeros((rows + 8, 8, ch), F32)
    ce[:, 64:72, :] = jnp.zeros((ce_rows, 8, ch), F32)
    fine[:, 64:72, :] = jnp.zeros((a_rows, 8, ch), F32)
    slope[:, 64:72, :] = jnp.zeros((a_rows, 8, ch), F32)
    gp[:, 64:72, :] = jnp.zeros((a_rows, 8, ch), F32)

    @pl.loop(0, rows // 4)
    def _(k):
        at = pl.ds(k * 4, 4)
        xf[pl.ds(4 + k * 4, 4), 4 : 4 + cols, :] = x_ref[at].astype(F32)
        ce[pl.ds(2 + k * 4, 4), 3 : 3 + cols, :] = ct_ref[at].astype(F32)

    for item in loads[2:]:
        item.wait()
    for k, ((dr, dc), _, _) in enumerate(plan):

        @pl.when(near(dr, dc))
        def _(k=k):
            edge(k).wait_send()

        @pl.when(near(-dr, -dc))
        def _(k=k):
            edge(k).wait_recv()

    def sides(dst, offset, at, lft, rgt, row_ok):
        ok_l, ok_r = has_left, has_right
        if row_ok is not None:
            ok_l = jnp.logical_and(ok_l, row_ok)
            ok_r = jnp.logical_and(ok_r, row_ok)
        rows_at = pl.ds(at, lft.shape[0])
        dst[rows_at, 0:offset, :] = jnp.where(ok_l, lft.astype(F32), 0.0)[:, 8 - offset : 8, :]
        dst[rows_at, offset + cols : offset + cols + 8, :] = jnp.where(ok_r, rgt.astype(F32), 0.0)

    xs, cs = slice(0, 8), slice(8, 16)
    for dst, offset, at, own, row_ok in (
        (xf, 4, 0, x_top, has_top),
        (xf, 4, rows + 4, x_bot, has_bot),
        (ce, 3, 0, ct_top, has_top),
        (ce, 3, rows + 2, ct_bot, has_bot),
    ):
        dst[at : at + own.shape[0], offset : offset + cols, :] = jnp.where(
            row_ok, own[...].astype(F32), 0.0
        )
    sides(xf, 4, 0, tl[:, xs, :], tr[:, xs, :], has_top)
    sides(xf, 4, rows + 4, bl[:, xs, :], br[:, xs, :], has_bot)
    sides(ce, 3, 0, tl[2:4, cs, :], tr[2:4, cs, :], has_top)
    sides(ce, 3, rows + 2, bl[0:2, cs, :], br[0:2, cs, :], has_bot)

    @pl.loop(0, rows // 8)
    def _(k):
        at = pl.ds(k * 8, 8)
        sides(xf, 4, 4 + k * 8, left[at, xs, :], right[at, xs, :], None)
        sides(ce, 3, 2 + k * 8, left[at, cs, :], right[at, cs, :], None)

    per_core = n_row * nz
    n_peers = n_row + nz - 1

    def stage_all(part, pieces_of):
        stage = parts[part][0]
        for row in range(n_row):
            for col in range(n_col):
                pieces = pieces_of(row * n_col + col)
                pad = stage.shape[1] - sum(p.shape[0] for p in pieces)
                if pad:
                    pieces.append(jnp.zeros((pad, 128), F32))
                slot = (col % 2) * per_core + row * nz + col // 2
                stage[slot] = jnp.concatenate(pieces, axis=0).astype(BF16)

    def sum_copies(part, level):
        stage, recv0, acc1, recv1, acc2, recv2 = parts[part]
        if level == 0:
            todo = [(0, stage.at[pl.ds((1 - core) * per_core, per_core)], recv0)]
        elif level == 1:
            todo = [(k, acc1.at[(r + k) % n_row], recv1.at[k - 1]) for k in range(1, n_row)]
        else:
            todo = [
                (n_row - 1 + k, acc2.at[(z + k) % nz], recv2.at[k - 1]) for k in range(1, nz)
            ]
        base = 10 + part * n_peers
        return [remote(base + k, src, dst, peers[k]) for k, src, dst in todo]

    def start_sums(part, level):
        if reduce:
            for item in sum_copies(part, level):
                item.start()

    def finish_sums(part, level):
        if not reduce:
            return None
        for item in sum_copies(part, level):
            item.wait()
        stage, recv0, acc1, recv1, acc2, recv2 = parts[part]
        if level == 0:
            for k in range(per_core):
                own = stage[core * per_core + k].astype(F32)
                acc1[k // nz, k % nz] = (own + recv0[k].astype(F32)).astype(BF16)
        elif level == 1:
            for k in range(nz):
                total = acc1[r, k].astype(F32)
                for m in range(n_row - 1):
                    total = total + recv1[m, k].astype(F32)
                acc2[k] = total.astype(BF16)
        else:
            total = acc2[z].astype(F32)
            for m in range(nz - 1):
                total = total + recv2[m].astype(F32)
            return total * scale
        return None

    parts = (refs[47:53], refs[53:59])
    scale = 1.0 / math.sqrt(rows * n_row * cols * n_col)
    blocks = n_row * n_col
    nc, nd, nu = 9 * ch // blocks, 9 * ch // blocks, 4 * wide // blocks

    @pl.loop(0, (rows + 8) // 4)
    def _(k):
        at = pl.ds(k * 4, 4)
        for q in range(3):
            x3[at, :, q * ch : (q + 1) * ch] = xf[at, q : q + 64, :].astype(BF16)

    wc_rows = wc[...].reshape(3, 3 * ch, ch)
    j_at = lax.broadcasted_iota(jnp.int32, (1, 64, 1), 1) - 3
    col_ok = jnp.logical_and(
        jnp.logical_or(j_at >= 0, has_left), jnp.logical_or(j_at < cols, has_right)
    )
    def in_grid(first, n):
        i_at = lax.broadcasted_iota(jnp.int32, (n, 1, 1), 0) + (first - 3)
        row_ok = jnp.logical_and(
            jnp.logical_or(i_at >= 0, has_top), jnp.logical_or(i_at < rows, has_bot)
        )
        return jnp.logical_and(row_ok, col_ok)

    step = a_rows // 2

    @pl.loop(0, 2)
    def _(k):
        pre = None
        for p in range(3):
            term = dot(x3[pl.ds(k * step + p, step)].reshape(step * 64, 3 * ch), wc_rows[p])
            pre = term if pre is None else pre + term
        sig = jax.nn.sigmoid(pre)
        at = pl.ds(k * step, step)
        ok = in_grid(k * step, step)
        value = (pre * sig).reshape(step, 64, ch)
        fine[at, 0:64, :] = jnp.where(ok, value, 0.0)
        slope[at, 0:64, :] = (sig * (1.0 + pre * (1.0 - sig))).reshape(step, 64, ch)

    @pl.loop(0, a_rows // 2)
    def _(k):
        for p in range(2):
            for q in range(3):
                d3[k, p, :, q * ch : (q + 1) * ch] = fine[
                    2 * k + p, pl.ds(q, 32, stride=2), :
                ].astype(BF16)

    @pl.loop(0, u_rows)
    def _(k):
        for p in range(2):
            for q in range(2):
                e = 2 * p + q
                t4[k, :, e * ch : (e + 1) * ch] = ce[
                    2 * k + p, pl.ds(1 + q, 32, stride=2), :
                ].astype(BF16)

    wd_rows = wd[...].reshape(3, 3 * ch, wide)
    cpre = None
    for p in range(3):
        window = d3[p // 2 : p // 2 + u_rows, p % 2].reshape(u_rows * 32, 3 * ch)
        term = dot(window, wd_rows[p])
        cpre = term if cpre is None else cpre + term
    cp[...] = cpre.reshape(u_rows, 32, wide)
    v_at = lax.broadcasted_iota(jnp.int32, (1, 32, 1), 1) - 1
    v_own = jnp.logical_and(v_at >= 0, v_at < cols // 2)
    sig = jax.nn.sigmoid(cp[...])
    co[...] = (cp[...] * sig).astype(BF16)
    grad = None
    for e in range(4):
        term = dot_nt(
            t4[:, :, e * ch : (e + 1) * ch].reshape(u_rows * 32, ch), wu[e // 2, e % 2]
        )
        grad = term if grad is None else grad + term
    u_at = lax.broadcasted_iota(jnp.int32, (u_rows, 1, 1), 0) - 1
    ok = jnp.logical_and(
        jnp.logical_and(jnp.logical_or(u_at >= 0, has_top), jnp.logical_or(u_at < half, has_bot)),
        jnp.logical_and(
            jnp.logical_or(v_at >= 0, has_left), jnp.logical_or(v_at < cols // 2, has_right)
        ),
    )
    full = cp[...]
    sig = jax.nn.sigmoid(full)
    part = grad.reshape(u_rows, 32, wide) * (sig * (1.0 + full * (1.0 - sig)))
    g[:, 32:40, :] = jnp.zeros((u_rows, 8, wide), F32)
    g[:, 0:32, :] = jnp.where(ok, part, 0.0)

    own_co = jnp.where(v_own, co[1 : half + 1].astype(F32), 0.0).astype(BF16)
    us = dot_tn(own_co.reshape(half * 32, wide), t4[1 : half + 1].reshape(half * 32, 4 * ch))
    for e in range(4):
        up_sum[e * wide : (e + 1) * wide, :] = us[:, e * ch : (e + 1) * ch]
    own_g = jnp.where(v_own, g[1 : half + 1, 0:32, :], 0.0).astype(BF16).reshape(half * 32, wide)
    for p in range(3):
        window = d3[p // 2 + 1 : p // 2 + 1 + half, p % 2].reshape(half * 32, 3 * ch)
        down_sum[p * 3 * ch : (p + 1) * 3 * ch, :] = dot_tn(window, own_g)

    if reduce:
        stage_all(
            0,
            lambda d: [
                up_sum[d * nu : (d + 1) * nu, :],
                down_sum[d * nd : (d + 1) * nd, 0:128],
                down_sum[d * nd : (d + 1) * nd, 128:256],
            ],
        )
    start_sums(0, 0)

    co_rows = co[1 : half + 1].reshape(half * 32, wide)
    for e in range(4):
        p, q = e // 2, e % 2
        res = dot(co_rows, wu[p, q]).reshape(half, 32, ch)
        for m in range(half):
            up[2 * m + p, pl.ds(1 + q, 32, stride=2), :] = res[m]

    @pl.loop(0, rows // 4)
    def _(k):
        f = fine[pl.ds(3 + k * 4, 4), 3 : 3 + cols, :].astype(BF16).astype(F32)
        out_ref[pl.ds(k * 4, 4)] = (f + up[pl.ds(k * 4, 4), 3 : 3 + cols, :]).astype(BF16)

    out_copy = pltpu.make_async_copy(out_ref, out_hbm, local_sem.at[5])
    out_copy.start()
    finish_sums(0, 0)
    start_sums(0, 1)

    g_here = g[:, 0:32, :].astype(BF16).reshape(u_rows * 32, wide)
    g_next = g[:, 1:33, :].astype(BF16).reshape(u_rows * 32, wide)
    less = (u_rows - 1) * 32

    def pair(p):
        return jnp.concatenate([wd[p, 1], wd[p, 2]], axis=0)

    even = dot_nt(g_here, pair(1))
    even_odd = even[:, ch:] + dot_nt(g_next, wd[1, 0])
    odd = dot_nt(g_here[32:], pair(0)) + dot_nt(g_here[:less], pair(2))
    odd_odd = odd[:, ch:] + dot_nt(g_next[32:], wd[0, 0]) + dot_nt(g_next[:less], wd[2, 0])
    spread = {
        (0, 0): even[:, :ch],
        (0, 1): even_odd,
        (1, 0): odd[:, :ch],
        (1, 1): odd_odd,
    }
    for (s, t), value in spread.items():
        for u in range(u_rows - s):
            at = pl.ds(1 + t, 32, stride=2)
            ce[2 * u + s, at, :] = ce[2 * u + s, at, :] + value[u * 32 : (u + 1) * 32]

    @pl.loop(0, (rows + 2) // 2)
    def _(k):
        a = 2 + 2 * k
        value = ce[pl.ds(a - 1, 2), 0:64, :] * slope[pl.ds(a, 2), 0:64, :]
        gp[pl.ds(a, 2), 0:64, :] = jnp.where(in_grid(a, 2), value, 0.0)

    @pl.loop(0, (rows + 2) // 2)
    def _(k):
        at = pl.ds(2 + 2 * k, 2)
        for q in range(3):
            g3[at, :, q * ch : (q + 1) * ch] = gp[at, 4 - q : 68 - q, :].astype(BF16)

    j_own = jnp.logical_and(j_at >= 0, j_at < cols)
    own = jnp.where(j_own, gp[3 : rows + 3, 0:64, :], 0.0).astype(BF16)

    def shift(p):
        pieces = [own]
        if p > 0:
            pieces.insert(0, jnp.zeros((p, 64, ch), BF16))
        if p < 2:
            pieces.append(jnp.zeros((2 - p, 64, ch), BF16))
        return jnp.concatenate(pieces, axis=0).reshape((rows + 2) * 64, ch)

    shifted = [shift(p) for p in range(3)]
    sums = dot_tn(
        x3[3 : rows + 5].reshape((rows + 2) * 64, 3 * ch), jnp.concatenate(shifted, axis=1)
    )
    for p in range(3):
        conv_sum[p * 3 * ch : (p + 1) * 3 * ch, :] = sums[:, p * ch : (p + 1) * ch]

    if reduce:
        stage_all(1, lambda d: [conv_sum[d * nc : (d + 1) * nc, :]])
    start_sums(1, 0)
    finish_sums(0, 1)
    start_sums(0, 2)

    turned = [jnp.concatenate([wc[p, q] for q in range(3)], axis=1) for p in range(3)]
    part_rows = rows // 2

    def half_inputs(k):
        total = None
        for p in range(3):
            first = k * part_rows + 4 - p
            window = g3[first : first + part_rows].reshape(part_rows * 64, 3 * ch)
            term = dot_nt(window, turned[p])
            total = term if total is None else total + term
        total = total.reshape(part_rows, 64, ch)[:, :cols, :]
        at = pl.ds(k * part_rows, part_rows)
        gx_ref[at] = total.astype(BF16)
        done = pltpu.make_async_copy(gx_ref.at[at], gx_hbm.at[at], local_sem.at[6 + k])
        done.start()
        return done

    first_half = half_inputs(0)
    finish_sums(1, 0)
    start_sums(1, 1)
    second_half = half_inputs(1)
    finish_sums(1, 1)
    start_sums(1, 2)
    total = finish_sums(0, 2)
    if reduce:
        up_out[...] = total[0:nu]
        down_out[:, 0:128] = total[nu : nu + nd]
        down_out[:, 128:256] = total[nu + nd : nu + 2 * nd]
    total = finish_sums(1, 2)
    if reduce:
        conv_out[...] = total[0:nc]
    for item in (out_copy, first_half, second_half):
        item.wait()


def body(n_row, n_col, x, ct, wc, wd, wu):
    rows, cols, ch = x.shape
    wide = wd.shape[3]
    a_rows, u_rows = rows + 6, rows // 2 + 2
    blocks, nz = n_row * n_col, n_col // 2
    sums = [(9 * ch, ch), (9 * ch, wide), (4 * wide, ch)]
    reduce = all(n % blocks == 0 for n, _ in sums)
    edges = [(4, cols, ch)] * 2 + [(2, cols, ch)] * 2 + [(rows, 16, ch)] * 2 + [(4, 16, ch)] * 4
    n_sems = 10
    scratch = [pltpu.VMEM(a.shape, BF16) for a in (x, ct, wc, wd, wu, x, x)]
    scratch += [pltpu.VMEM((2, rows, 16, ch), BF16)]
    scratch += [pltpu.VMEM(e, BF16) for e in edges]
    scratch += [
        pltpu.VMEM((rows + 8, 72, ch), F32),
        pltpu.VMEM((rows + 8, 64, 3 * ch), BF16),
        pltpu.VMEM((rows + 4, 72, ch), F32),
        pltpu.VMEM((a_rows, 72, ch), F32),
        pltpu.VMEM((a_rows, 72, ch), F32),
        pltpu.VMEM((a_rows // 2, 2, 32, 3 * ch), BF16),
        pltpu.VMEM((u_rows, 32, 4 * ch), BF16),
        pltpu.VMEM((u_rows, 32, wide), F32),
        pltpu.VMEM((u_rows, 32, wide), BF16),
        pltpu.VMEM((u_rows, 40, wide), F32),
        pltpu.VMEM((a_rows, 72, ch), F32),
        pltpu.VMEM((a_rows, 64, 3 * ch), BF16),
        pltpu.VMEM((rows, 72, ch), F32),
    ]
    more = []
    if reduce:
        n_sems += 2 * (n_row + nz - 1)
        more += [pltpu.VMEM(s, F32) for s in sums]
        heights = (sums[2][0] + 2 * sums[1][0]) // blocks, sums[0][0] // blocks
        for height in heights:
            height = -(-height // 16) * 16
            for lead in (
                (blocks,), (blocks // 2,), (n_row, nz), (n_row - 1, nz), (nz,), (nz - 1,)
            ):
                more.append(pltpu.VMEM(lead + (height, 128), BF16))
        outs = [(n // blocks, w) for n, w in sums]
    else:
        outs = sums
    scratch += [pltpu.SemaphoreType.DMA((n_sems,))] * 2 + [pltpu.SemaphoreType.DMA((8,))] + more
    anywhere = pl.BlockSpec(memory_space=pl.ANY)
    output, grad_inputs, *sums = pl.pallas_call(
        functools.partial(level_kernel, n_row, n_col, reduce),
        out_shape=[jax.ShapeDtypeStruct(x.shape, BF16)] * 2
        + [jax.ShapeDtypeStruct(s, F32) for s in outs],
        in_specs=[anywhere] * 5,
        out_specs=[anywhere] * 2 + [VMEM] * 3,
        scratch_shapes=scratch,
        compiler_params=pltpu.CompilerParams(
            collective_id=0, has_side_effects=True, vmem_limit_bytes=60 * 2**20
        ),
        name="level",
    )(x, ct, wc, wd, wu)
    sums = [a.reshape(-1) for a in sums]
    if not reduce:
        scale = 1.0 / math.sqrt(rows * n_row * cols * n_col)
        sums = [
            lax.psum_scatter(a, ("row", "col"), scatter_dimension=0, tiled=True) * scale
            for a in sums
        ]
    return (output, grad_inputs, *sums)


def solution(mesh):
    return jax.shard_map(
        functools.partial(body, mesh.shape["row"], mesh.shape["col"]),
        mesh=mesh,
        in_specs=(P("row", "col", None), P("row", "col", None), P(), P(), P()),
        out_specs=(
            P("row", "col", None),
            P("row", "col", None),
            P(("row", "col")),
            P(("row", "col")),
            P(("row", "col")),
        ),
        check_vma=False,
    )
```

```python
import functools
import math

import jax
import jax.numpy as jnp
from jax import lax
from jax.experimental import pallas as pl
from jax.experimental.pallas import tpu as pltpu
from jax.sharding import PartitionSpec as P

MESH = pl.DeviceIdType.MESH
F32 = jnp.float32
BF16 = jnp.bfloat16
VMEM = pl.BlockSpec(memory_space=pltpu.VMEM)
NT = (((1,), (1,)), ((), ()))
TN = (((0,), (0,)), ((), ()))
SHIFTS = [(dr, dc) for dr in (-1, 0, 1) for dc in (-1, 0, 1) if (dr, dc) != (0, 0)]


def dot(a, b):
    return jnp.dot(a, b, preferred_element_type=F32)


def dot_nt(a, b):
    return lax.dot_general(a, b, NT, preferred_element_type=F32)


def dot_tn(a, b):
    return lax.dot_general(a, b, TN, preferred_element_type=F32)


def exists(at, n, d):
    return at > 0 if d < 0 else at < n - 1


def level_kernel(n_row, n_col, reduce, *refs):
    x_hbm, ct_hbm, wc_hbm, wd_hbm, wu_hbm, out_hbm, gx_hbm, conv_out, down_out, up_out = refs[:10]
    x_ref, ct_ref, wc, wd, wu, out_ref, gx_ref, pack = refs[10:18]
    x_top, x_bot, ct_top, ct_bot, left, right, tl, tr, bl, br = edges = refs[18:28]
    (xf, x3, ce, fine, slope, d3, t4, cp, co, g, gp, g3, up) = refs[28:41]
    send_sem, recv_sem, local_sem = refs[41:44]
    conv_sum, down_sum, up_sum = refs[44:47] if reduce else (conv_out, down_out, up_out)
    rows, cols, ch = x_ref.shape
    wide = wd.shape[3]
    nz = n_col // 2
    r, c = lax.axis_index("row"), lax.axis_index("col")
    z, core = c // 2, c % 2
    has_top, has_bot = r > 0, r < n_row - 1
    has_left, has_right = c > 0, c < n_col - 1
    ce_rows, a_rows, u_rows = rows + 4, rows + 6, rows // 2 + 2
    half = rows // 2

    loads = [
        pltpu.make_async_copy(src, dst, local_sem.at[k])
        for k, (src, dst) in enumerate(
            [(x_hbm, x_ref), (ct_hbm, ct_ref), (wc_hbm, wc), (wd_hbm, wd), (wu_hbm, wu)]
        )
    ]
    for item in loads:
        item.start()

    def near(dr, dc):
        ok = None
        for d, at, n in ((dr, r, n_row), (dc, c, n_col)):
            if d:
                here = exists(at, n, d)
                ok = here if ok is None else jnp.logical_and(ok, here)
        return ok

    peers = [(r, z * 2 + 1 - core)]
    peers += [((r + k) % n_row, c) for k in range(1, n_row)]
    peers += [(r, ((z + k) % nz) * 2 + core) for k in range(1, nz)]
    if not reduce:
        peers = []
    barrier = pltpu.get_barrier_semaphore()
    for dr, dc in SHIFTS:

        @pl.when(near(dr, dc))
        def _(dr=dr, dc=dc):
            pl.semaphore_signal(barrier, inc=1, device_id=(r + dr, c + dc), device_id_type=MESH)

    for peer in peers:
        pl.semaphore_signal(barrier, inc=1, device_id=peer, device_id_type=MESH)

    loads[0].wait()
    loads[1].wait()
    for side, at in ((0, 0), (1, cols - 8)):
        pack[side] = jnp.concatenate(
            [x_ref[:, at : at + 8, :].astype(F32), ct_ref[:, at : at + 8, :].astype(F32)], axis=1
        ).astype(BF16)
    near_r = 3 - (r == 0).astype(jnp.int32) - (r == n_row - 1).astype(jnp.int32)
    near_c = 3 - (c == 0).astype(jnp.int32) - (c == n_col - 1).astype(jnp.int32)
    pl.semaphore_wait(barrier, near_r * near_c - 1 + len(peers))

    low, high = pl.ds(0, 4), pl.ds(rows - 4, 4)
    plan = [
        ((1, 0), x_ref.at[high], x_top),
        ((-1, 0), x_ref.at[low], x_bot),
        ((1, 0), ct_ref.at[pl.ds(rows - 2, 2)], ct_top),
        ((-1, 0), ct_ref.at[pl.ds(0, 2)], ct_bot),
        ((0, 1), pack.at[1], left),
        ((0, -1), pack.at[0], right),
        ((1, 1), pack.at[1, high], tl),
        ((1, -1), pack.at[0, high], tr),
        ((-1, 1), pack.at[1, low], bl),
        ((-1, -1), pack.at[0, low], br),
    ]

    def remote(k, src, dst, device):
        return pltpu.make_async_remote_copy(
            src_ref=src,
            dst_ref=dst,
            send_sem=send_sem.at[k],
            recv_sem=recv_sem.at[k],
            device_id=device,
            device_id_type=MESH,
        )

    def edge(k):
        (dr, dc), src, dst = plan[k]
        return remote(k, src, dst, (r + dr, c + dc))

    for k, ((dr, dc), _, _) in enumerate(plan):

        @pl.when(near(dr, dc))
        def _(k=k):
            edge(k).start()

    xf[:, 64:72, :] = jnp.zeros((rows + 8, 8, ch), F32)
    ce[:, 64:72, :] = jnp.zeros((ce_rows, 8, ch), F32)
    fine[:, 64:72, :] = jnp.zeros((a_rows, 8, ch), F32)
    slope[:, 64:72, :] = jnp.zeros((a_rows, 8, ch), F32)
    gp[:, 64:72, :] = jnp.zeros((a_rows, 8, ch), F32)

    @pl.loop(0, rows // 4)
    def _(k):
        at = pl.ds(k * 4, 4)
        xf[pl.ds(4 + k * 4, 4), 4 : 4 + cols, :] = x_ref[at].astype(F32)
        ce[pl.ds(2 + k * 4, 4), 3 : 3 + cols, :] = ct_ref[at].astype(F32)

    for item in loads[2:]:
        item.wait()
    for k, ((dr, dc), _, _) in enumerate(plan):

        @pl.when(near(dr, dc))
        def _(k=k):
            edge(k).wait_send()

        @pl.when(near(-dr, -dc))
        def _(k=k):
            edge(k).wait_recv()

    def sides(dst, offset, at, lft, rgt, row_ok):
        ok_l, ok_r = has_left, has_right
        if row_ok is not None:
            ok_l = jnp.logical_and(ok_l, row_ok)
            ok_r = jnp.logical_and(ok_r, row_ok)
        rows_at = pl.ds(at, lft.shape[0])
        dst[rows_at, 0:offset, :] = jnp.where(ok_l, lft.astype(F32), 0.0)[:, 8 - offset : 8, :]
        dst[rows_at, offset + cols : offset + cols + 8, :] = jnp.where(ok_r, rgt.astype(F32), 0.0)

    xs, cs = slice(0, 8), slice(8, 16)
    for dst, offset, at, own, row_ok in (
        (xf, 4, 0, x_top, has_top),
        (xf, 4, rows + 4, x_bot, has_bot),
        (ce, 3, 0, ct_top, has_top),
        (ce, 3, rows + 2, ct_bot, has_bot),
    ):
        dst[at : at + own.shape[0], offset : offset + cols, :] = jnp.where(
            row_ok, own[...].astype(F32), 0.0
        )
    sides(xf, 4, 0, tl[:, xs, :], tr[:, xs, :], has_top)
    sides(xf, 4, rows + 4, bl[:, xs, :], br[:, xs, :], has_bot)
    sides(ce, 3, 0, tl[2:4, cs, :], tr[2:4, cs, :], has_top)
    sides(ce, 3, rows + 2, bl[0:2, cs, :], br[0:2, cs, :], has_bot)

    @pl.loop(0, rows // 8)
    def _(k):
        at = pl.ds(k * 8, 8)
        sides(xf, 4, 4 + k * 8, left[at, xs, :], right[at, xs, :], None)
        sides(ce, 3, 2 + k * 8, left[at, cs, :], right[at, cs, :], None)

    per_core = n_row * nz
    n_peers = n_row + nz - 1

    def stage_all(part, pieces_of):
        stage = parts[part][0]
        for row in range(n_row):
            for col in range(n_col):
                pieces = pieces_of(row * n_col + col)
                pad = stage.shape[1] - sum(p.shape[0] for p in pieces)
                if pad:
                    pieces.append(jnp.zeros((pad, 128), F32))
                slot = (col % 2) * per_core + row * nz + col // 2
                stage[slot] = jnp.concatenate(pieces, axis=0).astype(BF16)

    def sum_copies(part, level):
        stage, recv0, acc1, recv1, acc2, recv2 = parts[part]
        if level == 0:
            todo = [(0, stage.at[pl.ds((1 - core) * per_core, per_core)], recv0)]
        elif level == 1:
            todo = [(k, acc1.at[(r + k) % n_row], recv1.at[k - 1]) for k in range(1, n_row)]
        else:
            todo = [
                (n_row - 1 + k, acc2.at[(z + k) % nz], recv2.at[k - 1]) for k in range(1, nz)
            ]
        base = 10 + part * n_peers
        return [remote(base + k, src, dst, peers[k]) for k, src, dst in todo]

    def start_sums(part, level):
        if reduce:
            for item in sum_copies(part, level):
                item.start()

    def finish_sums(part, level):
        if not reduce:
            return None
        for item in sum_copies(part, level):
            item.wait()
        stage, recv0, acc1, recv1, acc2, recv2 = parts[part]
        if level == 0:
            for k in range(per_core):
                own = stage[core * per_core + k].astype(F32)
                acc1[k // nz, k % nz] = (own + recv0[k].astype(F32)).astype(BF16)
        elif level == 1:
            for k in range(nz):
                total = acc1[r, k].astype(F32)
                for m in range(n_row - 1):
                    total = total + recv1[m, k].astype(F32)
                acc2[k] = total.astype(BF16)
        else:
            total = acc2[z].astype(F32)
            for m in range(nz - 1):
                total = total + recv2[m].astype(F32)
            return total * scale
        return None

    parts = (refs[47:53], refs[53:59])
    scale = 1.0 / math.sqrt(rows * n_row * cols * n_col)
    blocks = n_row * n_col
    nc, nd, nu = 9 * ch // blocks, 9 * ch // blocks, 4 * wide // blocks

    @pl.loop(0, (rows + 8) // 4)
    def _(k):
        at = pl.ds(k * 4, 4)
        for q in range(3):
            x3[at, :, q * ch : (q + 1) * ch] = xf[at, q : q + 64, :].astype(BF16)

    wc_rows = wc[...].reshape(3, 3 * ch, ch)
    j_at = lax.broadcasted_iota(jnp.int32, (1, 64, 1), 1) - 3
    col_ok = jnp.logical_and(
        jnp.logical_or(j_at >= 0, has_left), jnp.logical_or(j_at < cols, has_right)
    )
    def in_grid(first, n):
        i_at = lax.broadcasted_iota(jnp.int32, (n, 1, 1), 0) + (first - 3)
        row_ok = jnp.logical_and(
            jnp.logical_or(i_at >= 0, has_top), jnp.logical_or(i_at < rows, has_bot)
        )
        return jnp.logical_and(row_ok, col_ok)

    step = a_rows // 2

    @pl.loop(0, 2)
    def _(k):
        pre = None
        for p in range(3):
            term = dot(x3[pl.ds(k * step + p, step)].reshape(step * 64, 3 * ch), wc_rows[p])
            pre = term if pre is None else pre + term
        sig = jax.nn.sigmoid(pre)
        at = pl.ds(k * step, step)
        ok = in_grid(k * step, step)
        value = (pre * sig).reshape(step, 64, ch)
        fine[at, 0:64, :] = jnp.where(ok, value, 0.0)
        slope[at, 0:64, :] = (sig * (1.0 + pre * (1.0 - sig))).reshape(step, 64, ch)

    @pl.loop(0, a_rows // 2)
    def _(k):
        for p in range(2):
            for q in range(3):
                d3[k, p, :, q * ch : (q + 1) * ch] = fine[
                    2 * k + p, pl.ds(q, 32, stride=2), :
                ].astype(BF16)

    @pl.loop(0, u_rows)
    def _(k):
        for p in range(2):
            for q in range(2):
                e = 2 * p + q
                t4[k, :, e * ch : (e + 1) * ch] = ce[
                    2 * k + p, pl.ds(1 + q, 32, stride=2), :
                ].astype(BF16)

    wd_rows = wd[...].reshape(3, 3 * ch, wide)
    cpre = None
    for p in range(3):
        window = d3[p // 2 : p // 2 + u_rows, p % 2].reshape(u_rows * 32, 3 * ch)
        term = dot(window, wd_rows[p])
        cpre = term if cpre is None else cpre + term
    cp[...] = cpre.reshape(u_rows, 32, wide)
    v_at = lax.broadcasted_iota(jnp.int32, (1, 32, 1), 1) - 1
    v_own = jnp.logical_and(v_at >= 0, v_at < cols // 2)
    sig = jax.nn.sigmoid(cp[...])
    co[...] = (cp[...] * sig).astype(BF16)
    grad = None
    for e in range(4):
        term = dot_nt(
            t4[:, :, e * ch : (e + 1) * ch].reshape(u_rows * 32, ch), wu[e // 2, e % 2]
        )
        grad = term if grad is None else grad + term
    u_at = lax.broadcasted_iota(jnp.int32, (u_rows, 1, 1), 0) - 1
    ok = jnp.logical_and(
        jnp.logical_and(jnp.logical_or(u_at >= 0, has_top), jnp.logical_or(u_at < half, has_bot)),
        jnp.logical_and(
            jnp.logical_or(v_at >= 0, has_left), jnp.logical_or(v_at < cols // 2, has_right)
        ),
    )
    full = cp[...]
    sig = jax.nn.sigmoid(full)
    part = grad.reshape(u_rows, 32, wide) * (sig * (1.0 + full * (1.0 - sig)))
    g[:, 32:40, :] = jnp.zeros((u_rows, 8, wide), F32)
    g[:, 0:32, :] = jnp.where(ok, part, 0.0)

    own_co = jnp.where(v_own, co[1 : half + 1].astype(F32), 0.0).astype(BF16)
    us = dot_tn(own_co.reshape(half * 32, wide), t4[1 : half + 1].reshape(half * 32, 4 * ch))
    for e in range(4):
        up_sum[e * wide : (e + 1) * wide, :] = us[:, e * ch : (e + 1) * ch]
    own_g = jnp.where(v_own, g[1 : half + 1, 0:32, :], 0.0).astype(BF16).reshape(half * 32, wide)
    for p in range(3):
        window = d3[p // 2 + 1 : p // 2 + 1 + half, p % 2].reshape(half * 32, 3 * ch)
        down_sum[p * 3 * ch : (p + 1) * 3 * ch, :] = dot_tn(window, own_g)

    if reduce:
        stage_all(
            0,
            lambda d: [
                up_sum[d * nu : (d + 1) * nu, :],
                down_sum[d * nd : (d + 1) * nd, 0:128],
                down_sum[d * nd : (d + 1) * nd, 128:256],
            ],
        )
    start_sums(0, 0)

    g_here = g[:, 0:32, :].astype(BF16).reshape(u_rows * 32, wide)
    g_next = g[:, 1:33, :].astype(BF16).reshape(u_rows * 32, wide)
    less = (u_rows - 1) * 32

    def pair(p):
        return jnp.concatenate([wd[p, 1], wd[p, 2]], axis=0)

    even = dot_nt(g_here, pair(1))
    even_odd = even[:, ch:] + dot_nt(g_next, wd[1, 0])
    odd = dot_nt(g_here[32:], pair(0)) + dot_nt(g_here[:less], pair(2))
    odd_odd = odd[:, ch:] + dot_nt(g_next[32:], wd[0, 0]) + dot_nt(g_next[:less], wd[2, 0])
    spread = {
        (0, 0): even[:, :ch],
        (0, 1): even_odd,
        (1, 0): odd[:, :ch],
        (1, 1): odd_odd,
    }
    for (s, t), value in spread.items():
        for u in range(u_rows - s):
            at = pl.ds(1 + t, 32, stride=2)
            ce[2 * u + s, at, :] = ce[2 * u + s, at, :] + value[u * 32 : (u + 1) * 32]

    finish_sums(0, 0)
    start_sums(0, 1)

    @pl.loop(0, (rows + 2) // 2)
    def _(k):
        a = 2 + 2 * k
        value = ce[pl.ds(a - 1, 2), 0:64, :] * slope[pl.ds(a, 2), 0:64, :]
        gp[pl.ds(a, 2), 0:64, :] = jnp.where(in_grid(a, 2), value, 0.0)

    @pl.loop(0, (rows + 2) // 2)
    def _(k):
        at = pl.ds(2 + 2 * k, 2)
        for q in range(3):
            g3[at, :, q * ch : (q + 1) * ch] = gp[at, 4 - q : 68 - q, :].astype(BF16)

    j_own = jnp.logical_and(j_at >= 0, j_at < cols)
    own = jnp.where(j_own, gp[3 : rows + 3, 0:64, :], 0.0).astype(BF16)

    def shift(p):
        pieces = [own]
        if p > 0:
            pieces.insert(0, jnp.zeros((p, 64, ch), BF16))
        if p < 2:
            pieces.append(jnp.zeros((2 - p, 64, ch), BF16))
        return jnp.concatenate(pieces, axis=0).reshape((rows + 2) * 64, ch)

    shifted = [shift(p) for p in range(3)]
    sums = dot_tn(
        x3[3 : rows + 5].reshape((rows + 2) * 64, 3 * ch), jnp.concatenate(shifted, axis=1)
    )
    for p in range(3):
        conv_sum[p * 3 * ch : (p + 1) * 3 * ch, :] = sums[:, p * ch : (p + 1) * ch]

    if reduce:
        stage_all(1, lambda d: [conv_sum[d * nc : (d + 1) * nc, :]])
    start_sums(1, 0)

    co_rows = co[1 : half + 1].reshape(half * 32, wide)
    for e in range(4):
        p, q = e // 2, e % 2
        res = dot(co_rows, wu[p, q]).reshape(half, 32, ch)
        for m in range(half):
            up[2 * m + p, pl.ds(1 + q, 32, stride=2), :] = res[m]

    @pl.loop(0, rows // 4)
    def _(k):
        f = fine[pl.ds(3 + k * 4, 4), 3 : 3 + cols, :].astype(BF16).astype(F32)
        out_ref[pl.ds(k * 4, 4)] = (f + up[pl.ds(k * 4, 4), 3 : 3 + cols, :]).astype(BF16)

    out_copy = pltpu.make_async_copy(out_ref, out_hbm, local_sem.at[5])
    out_copy.start()
    finish_sums(1, 0)
    start_sums(1, 1)
    finish_sums(0, 1)
    start_sums(0, 2)

    turned = [jnp.concatenate([wc[p, q] for q in range(3)], axis=1) for p in range(3)]
    part_rows = rows // 2

    def half_inputs(k):
        total = None
        for p in range(3):
            first = k * part_rows + 4 - p
            window = g3[first : first + part_rows].reshape(part_rows * 64, 3 * ch)
            term = dot_nt(window, turned[p])
            total = term if total is None else total + term
        total = total.reshape(part_rows, 64, ch)[:, :cols, :]
        at = pl.ds(k * part_rows, part_rows)
        gx_ref[at] = total.astype(BF16)
        done = pltpu.make_async_copy(gx_ref.at[at], gx_hbm.at[at], local_sem.at[6 + k])
        done.start()
        return done

    first_half = half_inputs(0)
    finish_sums(1, 1)
    start_sums(1, 2)
    second_half = half_inputs(1)
    total = finish_sums(0, 2)
    if reduce:
        up_out[...] = total[0:nu]
        down_out[pl.ds(0, nd, stride=2), :] = total[nu : nu + nd]
        down_out[pl.ds(1, nd, stride=2), :] = total[nu + nd : nu + 2 * nd]
    total = finish_sums(1, 2)
    if reduce:
        conv_out[...] = total[0:nc]
    for item in (out_copy, first_half, second_half):
        item.wait()


def results_kernel(*refs):
    n = (len(refs) - 1) // 2
    copies = [pltpu.make_async_copy(refs[k], refs[n + k], refs[-1].at[k]) for k in range(n)]
    for item in copies:
        item.start()
    for item in copies:
        item.wait()


def results(arrays):
    anywhere = pl.BlockSpec(memory_space=pl.ANY)
    return pl.pallas_call(
        results_kernel,
        out_shape=[jax.ShapeDtypeStruct(a.shape, a.dtype) for a in arrays],
        in_specs=[anywhere] * len(arrays),
        out_specs=[anywhere] * len(arrays),
        scratch_shapes=[pltpu.SemaphoreType.DMA((len(arrays),))],
        compiler_params=pltpu.CompilerParams(vmem_limit_bytes=60 * 2**20),
        name="results",
    )(*arrays)


def body(n_row, n_col, x, ct, wc, wd, wu):
    rows, cols, ch = x.shape
    wide = wd.shape[3]
    a_rows, u_rows = rows + 6, rows // 2 + 2
    blocks, nz = n_row * n_col, n_col // 2
    sums = [(9 * ch, ch), (9 * ch, wide), (4 * wide, ch)]
    reduce = all(n % blocks == 0 for n, _ in sums)
    edges = [(4, cols, ch)] * 2 + [(2, cols, ch)] * 2 + [(rows, 16, ch)] * 2 + [(4, 16, ch)] * 4
    n_sems = 10
    scratch = [pltpu.VMEM(a.shape, BF16) for a in (x, ct, wc, wd, wu, x, x)]
    scratch += [pltpu.VMEM((2, rows, 16, ch), BF16)]
    scratch += [pltpu.VMEM(e, BF16) for e in edges]
    scratch += [
        pltpu.VMEM((rows + 8, 72, ch), F32),
        pltpu.VMEM((rows + 8, 64, 3 * ch), BF16),
        pltpu.VMEM((rows + 4, 72, ch), F32),
        pltpu.VMEM((a_rows, 72, ch), F32),
        pltpu.VMEM((a_rows, 72, ch), F32),
        pltpu.VMEM((a_rows // 2, 2, 32, 3 * ch), BF16),
        pltpu.VMEM((u_rows, 32, 4 * ch), BF16),
        pltpu.VMEM((u_rows, 32, wide), F32),
        pltpu.VMEM((u_rows, 32, wide), BF16),
        pltpu.VMEM((u_rows, 40, wide), F32),
        pltpu.VMEM((a_rows, 72, ch), F32),
        pltpu.VMEM((a_rows, 64, 3 * ch), BF16),
        pltpu.VMEM((rows, 72, ch), F32),
    ]
    more = []
    if reduce:
        n_sems += 2 * (n_row + nz - 1)
        more += [pltpu.VMEM(s, F32) for s in sums]
        heights = (sums[2][0] + 2 * sums[1][0]) // blocks, sums[0][0] // blocks
        for height in heights:
            height = -(-height // 16) * 16
            for lead in (
                (blocks,), (blocks // 2,), (n_row, nz), (n_row - 1, nz), (nz,), (nz - 1,)
            ):
                more.append(pltpu.VMEM(lead + (height, 128), BF16))
        outs = [(n * w // blocks // 128, 128) for n, w in sums]
    else:
        outs = sums
    scratch += [pltpu.SemaphoreType.DMA((n_sems,))] * 2 + [pltpu.SemaphoreType.DMA((8,))] + more
    anywhere = pl.BlockSpec(memory_space=pl.ANY)
    found = pl.pallas_call(
        functools.partial(level_kernel, n_row, n_col, reduce),
        out_shape=[jax.ShapeDtypeStruct(x.shape, BF16)] * 2
        + [jax.ShapeDtypeStruct(s, F32) for s in outs],
        in_specs=[anywhere] * 5,
        out_specs=[anywhere] * 2 + [VMEM] * 3,
        scratch_shapes=scratch,
        compiler_params=pltpu.CompilerParams(
            collective_id=0, has_side_effects=True, vmem_limit_bytes=60 * 2**20
        ),
        name="level",
    )(x, ct, wc, wd, wu)
    output, grad_inputs, *sums = results(found)
    sums = [a.reshape(-1) for a in sums]
    if not reduce:
        scale = 1.0 / math.sqrt(rows * n_row * cols * n_col)
        sums = [
            lax.psum_scatter(a, ("row", "col"), scatter_dimension=0, tiled=True) * scale
            for a in sums
        ]
    return (output, grad_inputs, *sums)


def solution(mesh):
    return jax.shard_map(
        functools.partial(body, mesh.shape["row"], mesh.shape["col"]),
        mesh=mesh,
        in_specs=(P("row", "col", None), P("row", "col", None), P(), P(), P()),
        out_specs=(
            P("row", "col", None),
            P("row", "col", None),
            P(("row", "col")),
            P(("row", "col")),
            P(("row", "col")),
        ),
        check_vma=False,
    )
```

```python
import functools
import math

import jax
import jax.numpy as jnp
from jax import lax
from jax.experimental import pallas as pl
from jax.experimental.pallas import tpu as pltpu
from jax.sharding import PartitionSpec as P

MESH = pl.DeviceIdType.MESH
F32 = jnp.float32
BF16 = jnp.bfloat16
VMEM = pl.BlockSpec(memory_space=pltpu.VMEM)
NT = (((1,), (1,)), ((), ()))
TN = (((0,), (0,)), ((), ()))
SHIFTS = [(dr, dc) for dr in (-1, 0, 1) for dc in (-1, 0, 1) if (dr, dc) != (0, 0)]


def dot(a, b):
    return jnp.dot(a, b, preferred_element_type=F32)


def dot_nt(a, b):
    return lax.dot_general(a, b, NT, preferred_element_type=F32)


def dot_tn(a, b):
    return lax.dot_general(a, b, TN, preferred_element_type=F32)


def exists(at, n, d):
    return at > 0 if d < 0 else at < n - 1


def level_kernel(n_row, n_col, reduce, *refs):
    x_hbm, ct_hbm, wc_hbm, wd_hbm, wu_hbm, out_hbm, gx_hbm, conv_out, down_out, up_out = refs[:10]
    x_ref, ct_ref, wc, wd, wu, out_ref, gx_ref, pack = refs[10:18]
    x_top, x_bot, ct_top, ct_bot, left, right, tl, tr, bl, br = edges = refs[18:28]
    (xf, x3, ce, fine, slope, d3, t4, cp, co, g, gp, g3, up) = refs[28:41]
    send_sem, recv_sem, local_sem = refs[41:44]
    conv_sum, down_sum, up_sum = refs[44:47] if reduce else (conv_out, down_out, up_out)
    rows, cols, ch = x_ref.shape
    wide = wd.shape[3]
    nz = n_col // 2
    r, c = lax.axis_index("row"), lax.axis_index("col")
    z, core = c // 2, c % 2
    has_top, has_bot = r > 0, r < n_row - 1
    has_left, has_right = c > 0, c < n_col - 1
    ce_rows, a_rows, u_rows = rows + 4, rows + 6, rows // 2 + 2
    half = rows // 2

    loads = [
        pltpu.make_async_copy(src, dst, local_sem.at[k])
        for k, (src, dst) in enumerate(
            [(x_hbm, x_ref), (ct_hbm, ct_ref), (wc_hbm, wc), (wd_hbm, wd), (wu_hbm, wu)]
        )
    ]

    def near(dr, dc):
        ok = None
        for d, at, n in ((dr, r, n_row), (dc, c, n_col)):
            if d:
                here = exists(at, n, d)
                ok = here if ok is None else jnp.logical_and(ok, here)
        return ok

    peers = [(r, z * 2 + 1 - core)]
    peers += [((r + k) % n_row, c) for k in range(1, n_row)]
    peers += [(r, ((z + k) % nz) * 2 + core) for k in range(1, nz)]
    if not reduce:
        peers = []
    barrier = pltpu.get_barrier_semaphore()
    for dr, dc in SHIFTS:

        @pl.when(near(dr, dc))
        def _(dr=dr, dc=dc):
            pl.semaphore_signal(barrier, inc=1, device_id=(r + dr, c + dc), device_id_type=MESH)

    for peer in peers:
        pl.semaphore_signal(barrier, inc=1, device_id=peer, device_id_type=MESH)

    for item in loads:
        item.start()

    loads[0].wait()
    loads[1].wait()
    for side, at in ((0, 0), (1, cols - 8)):
        pack[side] = jnp.concatenate(
            [x_ref[:, at : at + 8, :].astype(F32), ct_ref[:, at : at + 8, :].astype(F32)], axis=1
        ).astype(BF16)
    near_r = 3 - (r == 0).astype(jnp.int32) - (r == n_row - 1).astype(jnp.int32)
    near_c = 3 - (c == 0).astype(jnp.int32) - (c == n_col - 1).astype(jnp.int32)
    pl.semaphore_wait(barrier, near_r * near_c - 1 + len(peers))

    low, high = pl.ds(0, 4), pl.ds(rows - 4, 4)
    plan = [
        ((1, 0), x_ref.at[high], x_top),
        ((-1, 0), x_ref.at[low], x_bot),
        ((1, 0), ct_ref.at[pl.ds(rows - 2, 2)], ct_top),
        ((-1, 0), ct_ref.at[pl.ds(0, 2)], ct_bot),
        ((0, 1), pack.at[1], left),
        ((0, -1), pack.at[0], right),
        ((1, 1), pack.at[1, high], tl),
        ((1, -1), pack.at[0, high], tr),
        ((-1, 1), pack.at[1, low], bl),
        ((-1, -1), pack.at[0, low], br),
    ]

    def remote(k, src, dst, device):
        return pltpu.make_async_remote_copy(
            src_ref=src,
            dst_ref=dst,
            send_sem=send_sem.at[k],
            recv_sem=recv_sem.at[k],
            device_id=device,
            device_id_type=MESH,
        )

    def edge(k):
        (dr, dc), src, dst = plan[k]
        return remote(k, src, dst, (r + dr, c + dc))

    for k, ((dr, dc), _, _) in enumerate(plan):

        @pl.when(near(dr, dc))
        def _(k=k):
            edge(k).start()

    xf[:, 64:72, :] = jnp.zeros((rows + 8, 8, ch), F32)
    ce[:, 64:72, :] = jnp.zeros((ce_rows, 8, ch), F32)
    fine[:, 64:72, :] = jnp.zeros((a_rows, 8, ch), F32)
    slope[:, 64:72, :] = jnp.zeros((a_rows, 8, ch), F32)
    gp[:, 64:72, :] = jnp.zeros((a_rows, 8, ch), F32)

    def shift_inputs(at, first, n):
        for q in range(3):
            x3[at, first : first + n, q * ch : (q + 1) * ch] = xf[
                at, first + q : first + q + n, :
            ].astype(BF16)

    xf[:, 0:8, :] = jnp.zeros((rows + 8, 8, ch), F32)
    xf[:, 56:64, :] = jnp.zeros((rows + 8, 8, ch), F32)

    @pl.loop(0, rows // 4)
    def _(k):
        at = pl.ds(k * 4, 4)
        xf[pl.ds(4 + k * 4, 4), 4 : 4 + cols, :] = x_ref[at].astype(F32)
        ce[pl.ds(2 + k * 4, 4), 3 : 3 + cols, :] = ct_ref[at].astype(F32)
        shift_inputs(pl.ds(4 + k * 4, 4), 16, 32)

    for item in loads[2:]:
        item.wait()
    for k, ((dr, dc), _, _) in enumerate(plan):

        @pl.when(near(dr, dc))
        def _(k=k):
            edge(k).wait_send()

        @pl.when(near(-dr, -dc))
        def _(k=k):
            edge(k).wait_recv()

    def sides(dst, offset, at, lft, rgt, row_ok):
        ok_l, ok_r = has_left, has_right
        if row_ok is not None:
            ok_l = jnp.logical_and(ok_l, row_ok)
            ok_r = jnp.logical_and(ok_r, row_ok)
        rows_at = pl.ds(at, lft.shape[0])
        dst[rows_at, 0:offset, :] = jnp.where(ok_l, lft.astype(F32), 0.0)[:, 8 - offset : 8, :]
        dst[rows_at, offset + cols : offset + cols + 8, :] = jnp.where(ok_r, rgt.astype(F32), 0.0)

    xs, cs = slice(0, 8), slice(8, 16)
    for dst, offset, at, own, row_ok in (
        (xf, 4, 0, x_top, has_top),
        (xf, 4, rows + 4, x_bot, has_bot),
        (ce, 3, 0, ct_top, has_top),
        (ce, 3, rows + 2, ct_bot, has_bot),
    ):
        dst[at : at + own.shape[0], offset : offset + cols, :] = jnp.where(
            row_ok, own[...].astype(F32), 0.0
        )
    sides(xf, 4, 0, tl[:, xs, :], tr[:, xs, :], has_top)
    sides(xf, 4, rows + 4, bl[:, xs, :], br[:, xs, :], has_bot)
    sides(ce, 3, 0, tl[2:4, cs, :], tr[2:4, cs, :], has_top)
    sides(ce, 3, rows + 2, bl[0:2, cs, :], br[0:2, cs, :], has_bot)

    @pl.loop(0, rows // 8)
    def _(k):
        at = pl.ds(k * 8, 8)
        sides(xf, 4, 4 + k * 8, left[at, xs, :], right[at, xs, :], None)
        sides(ce, 3, 2 + k * 8, left[at, cs, :], right[at, cs, :], None)

    per_core = n_row * nz
    n_peers = n_row + nz - 1

    def stage_all(part, pieces_of):
        stage = parts[part][0]
        for row in range(n_row):
            for col in range(n_col):
                pieces = pieces_of(row * n_col + col)
                pad = stage.shape[1] - sum(p.shape[0] for p in pieces)
                if pad:
                    pieces.append(jnp.zeros((pad, 128), F32))
                slot = (col % 2) * per_core + row * nz + col // 2
                stage[slot] = jnp.concatenate(pieces, axis=0).astype(BF16)

    def sum_copies(part, level):
        stage, recv0, acc1, recv1, acc2, recv2 = parts[part]
        if level == 0:
            todo = [(0, stage.at[pl.ds((1 - core) * per_core, per_core)], recv0)]
        elif level == 1:
            todo = [(k, acc1.at[(r + k) % n_row], recv1.at[k - 1]) for k in range(1, n_row)]
        else:
            todo = [
                (n_row - 1 + k, acc2.at[(z + k) % nz], recv2.at[k - 1]) for k in range(1, nz)
            ]
        base = 10 + part * n_peers
        return [remote(base + k, src, dst, peers[k]) for k, src, dst in todo]

    def start_sums(part, level):
        if reduce:
            for item in sum_copies(part, level):
                item.start()

    def finish_sums(part, level):
        if not reduce:
            return None
        for item in sum_copies(part, level):
            item.wait()
        stage, recv0, acc1, recv1, acc2, recv2 = parts[part]
        if level == 0:
            for k in range(per_core):
                own = stage[core * per_core + k].astype(F32)
                acc1[k // nz, k % nz] = (own + recv0[k].astype(F32)).astype(BF16)
        elif level == 1:
            for k in range(nz):
                total = acc1[r, k].astype(F32)
                for m in range(n_row - 1):
                    total = total + recv1[m, k].astype(F32)
                acc2[k] = total.astype(BF16)
        else:
            total = acc2[z].astype(F32)
            for m in range(nz - 1):
                total = total + recv2[m].astype(F32)
            return total * scale
        return None

    parts = (refs[47:53], refs[53:59])
    scale = 1.0 / math.sqrt(rows * n_row * cols * n_col)
    blocks = n_row * n_col
    nc, nd, nu = 9 * ch // blocks, 9 * ch // blocks, 4 * wide // blocks

    for at in (pl.ds(0, 4), pl.ds(rows + 4, 4)):
        shift_inputs(at, 0, 64)

    @pl.loop(0, rows // 8)
    def _(k):
        at = pl.ds(4 + k * 8, 8)
        shift_inputs(at, 0, 16)
        shift_inputs(at, 48, 16)

    wc_rows = wc[...].reshape(9 * ch, ch)
    j_at = lax.broadcasted_iota(jnp.int32, (1, 64, 1), 1) - 3
    col_ok = jnp.logical_and(
        jnp.logical_or(j_at >= 0, has_left), jnp.logical_or(j_at < cols, has_right)
    )
    def in_grid(first, n):
        i_at = lax.broadcasted_iota(jnp.int32, (n, 1, 1), 0) + (first - 3)
        row_ok = jnp.logical_and(
            jnp.logical_or(i_at >= 0, has_top), jnp.logical_or(i_at < rows, has_bot)
        )
        return jnp.logical_and(row_ok, col_ok)

    step = a_rows // 2

    @pl.loop(0, 2)
    def _(k):
        windows = [
            x3[pl.ds(k * step + p, step)].reshape(step * 64, 3 * ch) for p in range(3)
        ]
        pre = dot(jnp.concatenate(windows, axis=1), wc_rows)
        sig = jax.nn.sigmoid(pre)
        at = pl.ds(k * step, step)
        ok = in_grid(k * step, step)
        value = (pre * sig).reshape(step, 64, ch)
        fine[at, 0:64, :] = jnp.where(ok, value, 0.0)
        slope[at, 0:64, :] = (sig * (1.0 + pre * (1.0 - sig))).reshape(step, 64, ch)

    @pl.loop(0, a_rows // 2)
    def _(k):
        for p in range(2):
            for q in range(3):
                d3[k, p, :, q * ch : (q + 1) * ch] = fine[
                    2 * k + p, pl.ds(q, 32, stride=2), :
                ].astype(BF16)

    @pl.loop(0, u_rows)
    def _(k):
        for p in range(2):
            for q in range(2):
                e = 2 * p + q
                t4[k, :, e * ch : (e + 1) * ch] = ce[
                    2 * k + p, pl.ds(1 + q, 32, stride=2), :
                ].astype(BF16)

    windows = [
        d3[p // 2 : p // 2 + u_rows, p % 2].reshape(u_rows * 32, 3 * ch) for p in range(3)
    ]
    cpre = dot(jnp.concatenate(windows, axis=1), wd[...].reshape(9 * ch, wide))
    cp[...] = cpre.reshape(u_rows, 32, wide)
    v_at = lax.broadcasted_iota(jnp.int32, (1, 32, 1), 1) - 1
    v_own = jnp.logical_and(v_at >= 0, v_at < cols // 2)
    sig = jax.nn.sigmoid(cp[...])
    co[...] = (cp[...] * sig).astype(BF16)
    grad = None
    for e in range(4):
        term = dot_nt(
            t4[:, :, e * ch : (e + 1) * ch].reshape(u_rows * 32, ch), wu[e // 2, e % 2]
        )
        grad = term if grad is None else grad + term
    u_at = lax.broadcasted_iota(jnp.int32, (u_rows, 1, 1), 0) - 1
    ok = jnp.logical_and(
        jnp.logical_and(jnp.logical_or(u_at >= 0, has_top), jnp.logical_or(u_at < half, has_bot)),
        jnp.logical_and(
            jnp.logical_or(v_at >= 0, has_left), jnp.logical_or(v_at < cols // 2, has_right)
        ),
    )
    full = cp[...]
    sig = jax.nn.sigmoid(full)
    part = grad.reshape(u_rows, 32, wide) * (sig * (1.0 + full * (1.0 - sig)))
    g[:, 32:40, :] = jnp.zeros((u_rows, 8, wide), F32)
    g[:, 0:32, :] = jnp.where(ok, part, 0.0)

    own_co = jnp.where(v_own, co[1 : half + 1].astype(F32), 0.0).astype(BF16)
    us = dot_tn(own_co.reshape(half * 32, wide), t4[1 : half + 1].reshape(half * 32, 4 * ch))
    for e in range(4):
        up_sum[e * wide : (e + 1) * wide, :] = us[:, e * ch : (e + 1) * ch]
    own_g = jnp.where(v_own, g[1 : half + 1, 0:32, :], 0.0).astype(BF16).reshape(half * 32, wide)
    for p in range(3):
        window = d3[p // 2 + 1 : p // 2 + 1 + half, p % 2].reshape(half * 32, 3 * ch)
        down_sum[p * 3 * ch : (p + 1) * 3 * ch, :] = dot_tn(window, own_g)

    if reduce:
        stage_all(
            0,
            lambda d: [
                up_sum[d * nu : (d + 1) * nu, :],
                down_sum[d * nd : (d + 1) * nd, 0:128],
                down_sum[d * nd : (d + 1) * nd, 128:256],
            ],
        )
    start_sums(0, 0)

    g_here = g[:, 0:32, :].astype(BF16).reshape(u_rows * 32, wide)
    g_next = g[:, 1:33, :].astype(BF16).reshape(u_rows * 32, wide)
    less = (u_rows - 1) * 32

    def pair(p):
        return jnp.concatenate([wd[p, 1], wd[p, 2]], axis=0)

    even = dot_nt(g_here, pair(1))
    even_odd = even[:, ch:] + dot_nt(g_next, wd[1, 0])
    odd = dot_nt(g_here[32:], pair(0)) + dot_nt(g_here[:less], pair(2))
    odd_odd = odd[:, ch:] + dot_nt(g_next[32:], wd[0, 0]) + dot_nt(g_next[:less], wd[2, 0])
    spread = {
        (0, 0): even[:, :ch],
        (0, 1): even_odd,
        (1, 0): odd[:, :ch],
        (1, 1): odd_odd,
    }
    for (s, t), value in spread.items():
        for u in range(u_rows - s):
            at = pl.ds(1 + t, 32, stride=2)
            ce[2 * u + s, at, :] = ce[2 * u + s, at, :] + value[u * 32 : (u + 1) * 32]

    finish_sums(0, 0)
    start_sums(0, 1)

    @pl.loop(0, (rows + 2) // 2)
    def _(k):
        a = 2 + 2 * k
        value = ce[pl.ds(a - 1, 2), 0:64, :] * slope[pl.ds(a, 2), 0:64, :]
        gp[pl.ds(a, 2), 0:64, :] = jnp.where(in_grid(a, 2), value, 0.0)

    @pl.loop(0, (rows + 2) // 2)
    def _(k):
        at = pl.ds(2 + 2 * k, 2)
        for q in range(3):
            g3[at, :, q * ch : (q + 1) * ch] = gp[at, 4 - q : 68 - q, :].astype(BF16)

    j_own = jnp.logical_and(j_at >= 0, j_at < cols)
    own = jnp.where(j_own, gp[3 : rows + 3, 0:64, :], 0.0).astype(BF16)

    def shift(p):
        pieces = [own]
        if p > 0:
            pieces.insert(0, jnp.zeros((p, 64, ch), BF16))
        if p < 2:
            pieces.append(jnp.zeros((2 - p, 64, ch), BF16))
        return jnp.concatenate(pieces, axis=0).reshape((rows + 2) * 64, ch)

    shifted = [shift(p) for p in range(3)]
    sums = dot_tn(
        x3[3 : rows + 5].reshape((rows + 2) * 64, 3 * ch), jnp.concatenate(shifted, axis=1)
    )
    for p in range(3):
        conv_sum[p * 3 * ch : (p + 1) * 3 * ch, :] = sums[:, p * ch : (p + 1) * ch]

    if reduce:
        stage_all(1, lambda d: [conv_sum[d * nc : (d + 1) * nc, :]])
    start_sums(1, 0)

    co_rows = co[1 : half + 1].reshape(half * 32, wide)
    for e in range(4):
        p, q = e // 2, e % 2
        res = dot(co_rows, wu[p, q]).reshape(half, 32, ch)
        for m in range(half):
            up[2 * m + p, pl.ds(1 + q, 32, stride=2), :] = res[m]

    @pl.loop(0, rows // 4)
    def _(k):
        f = fine[pl.ds(3 + k * 4, 4), 3 : 3 + cols, :].astype(BF16).astype(F32)
        out_ref[pl.ds(k * 4, 4)] = (f + up[pl.ds(k * 4, 4), 3 : 3 + cols, :]).astype(BF16)

    out_copy = pltpu.make_async_copy(out_ref, out_hbm, local_sem.at[5])
    out_copy.start()
    finish_sums(1, 0)
    start_sums(1, 1)
    finish_sums(0, 1)
    start_sums(0, 2)

    turned = jnp.concatenate([wc[p, q] for p in range(3) for q in range(3)], axis=1)
    part_rows = rows // 2

    def half_inputs(k):
        windows = [
            g3[k * part_rows + 4 - p : (k + 1) * part_rows + 4 - p].reshape(
                part_rows * 64, 3 * ch
            )
            for p in range(3)
        ]
        total = dot_nt(jnp.concatenate(windows, axis=1), turned)
        total = total.reshape(part_rows, 64, ch)[:, :cols, :]
        at = pl.ds(k * part_rows, part_rows)
        gx_ref[at] = total.astype(BF16)
        done = pltpu.make_async_copy(gx_ref.at[at], gx_hbm.at[at], local_sem.at[6 + k])
        done.start()
        return done

    first_half = half_inputs(0)
    finish_sums(1, 1)
    start_sums(1, 2)
    second_half = half_inputs(1)
    total = finish_sums(0, 2)
    if reduce:
        up_out[...] = total[0:nu]
        down_out[pl.ds(0, nd, stride=2), :] = total[nu : nu + nd]
        down_out[pl.ds(1, nd, stride=2), :] = total[nu + nd : nu + 2 * nd]
    total = finish_sums(1, 2)
    if reduce:
        conv_out[...] = total[0:nc]
    for item in (out_copy, first_half, second_half):
        item.wait()


def results_kernel(n, *refs):
    given, out, held, (in_sem, out_sem) = refs[:n], refs[n : 2 * n], refs[2 * n : 3 * n], refs[3 * n :]
    pieces = []
    for k in range(n):
        size = given[k].shape[0]
        step = size // 2 if len(given[k].shape) == 3 else size
        pieces += [(k, pl.ds(at, step)) for at in range(0, size, step)]
    loads = [
        pltpu.make_async_copy(given[k].at[at], held[k].at[at], in_sem.at[m])
        for m, (k, at) in enumerate(pieces)
    ]
    stores = [
        pltpu.make_async_copy(held[k].at[at], out[k].at[at], out_sem.at[m])
        for m, (k, at) in enumerate(pieces)
    ]
    for item in loads:
        item.start()
    for load, store in zip(loads, stores):
        load.wait()
        store.start()
    for item in stores:
        item.wait()


def results(arrays):
    anywhere = pl.BlockSpec(memory_space=pl.ANY)
    n = len(arrays)
    return pl.pallas_call(
        functools.partial(results_kernel, n),
        out_shape=[jax.ShapeDtypeStruct(a.shape, a.dtype) for a in arrays],
        in_specs=[anywhere] * n,
        out_specs=[anywhere] * n,
        scratch_shapes=[pltpu.VMEM(a.shape, a.dtype) for a in arrays]
        + [pltpu.SemaphoreType.DMA((2 * n,))] * 2,
        compiler_params=pltpu.CompilerParams(vmem_limit_bytes=60 * 2**20),
        name="results",
    )(*arrays)


def body(n_row, n_col, x, ct, wc, wd, wu):
    rows, cols, ch = x.shape
    wide = wd.shape[3]
    a_rows, u_rows = rows + 6, rows // 2 + 2
    blocks, nz = n_row * n_col, n_col // 2
    sums = [(9 * ch, ch), (9 * ch, wide), (4 * wide, ch)]
    reduce = all(n % blocks == 0 for n, _ in sums)
    edges = [(4, cols, ch)] * 2 + [(2, cols, ch)] * 2 + [(rows, 16, ch)] * 2 + [(4, 16, ch)] * 4
    n_sems = 10
    scratch = [pltpu.VMEM(a.shape, BF16) for a in (x, ct, wc, wd, wu, x, x)]
    scratch += [pltpu.VMEM((2, rows, 16, ch), BF16)]
    scratch += [pltpu.VMEM(e, BF16) for e in edges]
    scratch += [
        pltpu.VMEM((rows + 8, 72, ch), F32),
        pltpu.VMEM((rows + 8, 64, 3 * ch), BF16),
        pltpu.VMEM((rows + 4, 72, ch), F32),
        pltpu.VMEM((a_rows, 72, ch), F32),
        pltpu.VMEM((a_rows, 72, ch), F32),
        pltpu.VMEM((a_rows // 2, 2, 32, 3 * ch), BF16),
        pltpu.VMEM((u_rows, 32, 4 * ch), BF16),
        pltpu.VMEM((u_rows, 32, wide), F32),
        pltpu.VMEM((u_rows, 32, wide), BF16),
        pltpu.VMEM((u_rows, 40, wide), F32),
        pltpu.VMEM((a_rows, 72, ch), F32),
        pltpu.VMEM((a_rows, 64, 3 * ch), BF16),
        pltpu.VMEM((rows, 72, ch), F32),
    ]
    more = []
    if reduce:
        n_sems += 2 * (n_row + nz - 1)
        more += [pltpu.VMEM(s, F32) for s in sums]
        heights = (sums[2][0] + 2 * sums[1][0]) // blocks, sums[0][0] // blocks
        for height in heights:
            height = -(-height // 16) * 16
            for lead in (
                (blocks,), (blocks // 2,), (n_row, nz), (n_row - 1, nz), (nz,), (nz - 1,)
            ):
                more.append(pltpu.VMEM(lead + (height, 128), BF16))
        outs = [(n * w // blocks // 128, 128) for n, w in sums]
    else:
        outs = sums
    scratch += [pltpu.SemaphoreType.DMA((n_sems,))] * 2 + [pltpu.SemaphoreType.DMA((8,))] + more
    anywhere = pl.BlockSpec(memory_space=pl.ANY)
    found = pl.pallas_call(
        functools.partial(level_kernel, n_row, n_col, reduce),
        out_shape=[jax.ShapeDtypeStruct(x.shape, BF16)] * 2
        + [jax.ShapeDtypeStruct(s, F32) for s in outs],
        in_specs=[anywhere] * 5,
        out_specs=[anywhere] * 2 + [VMEM] * 3,
        scratch_shapes=scratch,
        compiler_params=pltpu.CompilerParams(
            collective_id=0, has_side_effects=True, vmem_limit_bytes=60 * 2**20
        ),
        name="level",
    )(x, ct, wc, wd, wu)
    output, grad_inputs, *sums = results(found)
    sums = [a.reshape(-1) for a in sums]
    if not reduce:
        scale = 1.0 / math.sqrt(rows * n_row * cols * n_col)
        sums = [
            lax.psum_scatter(a, ("row", "col"), scatter_dimension=0, tiled=True) * scale
            for a in sums
        ]
    return (output, grad_inputs, *sums)


def solution(mesh):
    return jax.shard_map(
        functools.partial(body, mesh.shape["row"], mesh.shape["col"]),
        mesh=mesh,
        in_specs=(P("row", "col", None), P("row", "col", None), P(), P(), P()),
        out_specs=(
            P("row", "col", None),
            P("row", "col", None),
            P(("row", "col")),
            P(("row", "col")),
            P(("row", "col")),
        ),
        check_vma=False,
    )
```

```python
import functools
import math

import jax
import jax.numpy as jnp
from jax import lax
from jax.experimental import pallas as pl
from jax.experimental.pallas import tpu as pltpu
from jax.sharding import PartitionSpec as P

MESH = pl.DeviceIdType.MESH
F32 = jnp.float32
BF16 = jnp.bfloat16
VMEM = pl.BlockSpec(memory_space=pltpu.VMEM)
NT = (((1,), (1,)), ((), ()))
TN = (((0,), (0,)), ((), ()))
SHIFTS = [(dr, dc) for dr in (-1, 0, 1) for dc in (-1, 0, 1) if (dr, dc) != (0, 0)]


def dot(a, b):
    return jnp.dot(a, b, preferred_element_type=F32)


def dot_nt(a, b):
    return lax.dot_general(a, b, NT, preferred_element_type=F32)


def dot_tn(a, b):
    return lax.dot_general(a, b, TN, preferred_element_type=F32)


def exists(at, n, d):
    return at > 0 if d < 0 else at < n - 1


def level_kernel(n_row, n_col, reduce, *refs):
    x_hbm, ct_hbm, wc_hbm, wd_hbm, wu_hbm, out_hbm, gx_hbm, conv_out, down_out, up_out = refs[:10]
    x_ref, ct_ref, wc, wd, wu, out_ref, gx_ref, pack = refs[10:18]
    x_top, x_bot, ct_top, ct_bot, left, right, tl, tr, bl, br = edges = refs[18:28]
    (xf, x3, ce, fine, slope, d3, t4, cp, co, g, gp, g3, up) = refs[28:41]
    send_sem, recv_sem, local_sem = refs[41:44]
    conv_sum, down_sum, up_sum = refs[44:47] if reduce else (conv_out, down_out, up_out)
    rows, cols, ch = x_ref.shape
    wide = wd.shape[3]
    nz = n_col // 2
    r, c = lax.axis_index("row"), lax.axis_index("col")
    z, core = c // 2, c % 2
    has_top, has_bot = r > 0, r < n_row - 1
    has_left, has_right = c > 0, c < n_col - 1
    ce_rows, a_rows, u_rows = rows + 4, rows + 6, rows // 2 + 2
    half = rows // 2

    loads = [
        pltpu.make_async_copy(src, dst, local_sem.at[k])
        for k, (src, dst) in enumerate(
            [(x_hbm, x_ref), (ct_hbm, ct_ref), (wc_hbm, wc), (wd_hbm, wd), (wu_hbm, wu)]
        )
    ]

    def near(dr, dc):
        ok = None
        for d, at, n in ((dr, r, n_row), (dc, c, n_col)):
            if d:
                here = exists(at, n, d)
                ok = here if ok is None else jnp.logical_and(ok, here)
        return ok

    peers = [(r, z * 2 + 1 - core)]
    peers += [((r + k) % n_row, c) for k in range(1, n_row)]
    peers += [(r, ((z + k) % nz) * 2 + core) for k in range(1, nz)]
    if not reduce:
        peers = []
    barrier = pltpu.get_barrier_semaphore()
    for dr, dc in SHIFTS:

        @pl.when(near(dr, dc))
        def _(dr=dr, dc=dc):
            pl.semaphore_signal(barrier, inc=1, device_id=(r + dr, c + dc), device_id_type=MESH)

    for peer in peers:
        pl.semaphore_signal(barrier, inc=1, device_id=peer, device_id_type=MESH)

    for item in loads:
        item.start()

    loads[0].wait()
    loads[1].wait()
    for side, at in ((0, 0), (1, cols - 8)):
        pack[side] = jnp.concatenate(
            [x_ref[:, at : at + 8, :].astype(F32), ct_ref[:, at : at + 8, :].astype(F32)], axis=1
        ).astype(BF16)
    near_r = 3 - (r == 0).astype(jnp.int32) - (r == n_row - 1).astype(jnp.int32)
    near_c = 3 - (c == 0).astype(jnp.int32) - (c == n_col - 1).astype(jnp.int32)
    pl.semaphore_wait(barrier, near_r * near_c - 1 + len(peers))

    low, high = pl.ds(0, 4), pl.ds(rows - 4, 4)
    plan = [
        ((1, 0), x_ref.at[high], x_top),
        ((-1, 0), x_ref.at[low], x_bot),
        ((1, 0), ct_ref.at[pl.ds(rows - 2, 2)], ct_top),
        ((-1, 0), ct_ref.at[pl.ds(0, 2)], ct_bot),
        ((0, 1), pack.at[1], left),
        ((0, -1), pack.at[0], right),
        ((1, 1), pack.at[1, high], tl),
        ((1, -1), pack.at[0, high], tr),
        ((-1, 1), pack.at[1, low], bl),
        ((-1, -1), pack.at[0, low], br),
    ]

    def remote(k, src, dst, device):
        return pltpu.make_async_remote_copy(
            src_ref=src,
            dst_ref=dst,
            send_sem=send_sem.at[k],
            recv_sem=recv_sem.at[k],
            device_id=device,
            device_id_type=MESH,
        )

    def edge(k):
        (dr, dc), src, dst = plan[k]
        return remote(k, src, dst, (r + dr, c + dc))

    for k, ((dr, dc), _, _) in enumerate(plan):

        @pl.when(near(dr, dc))
        def _(k=k):
            edge(k).start()

    xf[:, 64:72, :] = jnp.zeros((rows + 8, 8, ch), F32)
    ce[:, 64:72, :] = jnp.zeros((ce_rows, 8, ch), F32)
    fine[:, 64:72, :] = jnp.zeros((a_rows, 8, ch), F32)
    slope[:, 64:72, :] = jnp.zeros((a_rows, 8, ch), F32)
    gp[:, 64:72, :] = jnp.zeros((a_rows, 8, ch), F32)

    def shift_inputs(at, first, n):
        for q in range(3):
            x3[at, first : first + n, q * ch : (q + 1) * ch] = xf[
                at, first + q : first + q + n, :
            ].astype(BF16)

    xf[:, 0:8, :] = jnp.zeros((rows + 8, 8, ch), F32)
    xf[:, 56:64, :] = jnp.zeros((rows + 8, 8, ch), F32)

    @pl.loop(0, rows // 4)
    def _(k):
        at = pl.ds(k * 4, 4)
        xf[pl.ds(4 + k * 4, 4), 4 : 4 + cols, :] = x_ref[at].astype(F32)
        ce[pl.ds(2 + k * 4, 4), 3 : 3 + cols, :] = ct_ref[at].astype(F32)
        shift_inputs(pl.ds(4 + k * 4, 4), 16, 32)

    for item in loads[2:]:
        item.wait()
    for k, ((dr, dc), _, _) in enumerate(plan):

        @pl.when(near(dr, dc))
        def _(k=k):
            edge(k).wait_send()

        @pl.when(near(-dr, -dc))
        def _(k=k):
            edge(k).wait_recv()

    def sides(dst, offset, at, lft, rgt, row_ok):
        ok_l, ok_r = has_left, has_right
        if row_ok is not None:
            ok_l = jnp.logical_and(ok_l, row_ok)
            ok_r = jnp.logical_and(ok_r, row_ok)
        rows_at = pl.ds(at, lft.shape[0])
        dst[rows_at, 0:offset, :] = jnp.where(ok_l, lft.astype(F32), 0.0)[:, 8 - offset : 8, :]
        dst[rows_at, offset + cols : offset + cols + 8, :] = jnp.where(ok_r, rgt.astype(F32), 0.0)

    xs, cs = slice(0, 8), slice(8, 16)
    for dst, offset, at, own, row_ok in (
        (xf, 4, 0, x_top, has_top),
        (xf, 4, rows + 4, x_bot, has_bot),
        (ce, 3, 0, ct_top, has_top),
        (ce, 3, rows + 2, ct_bot, has_bot),
    ):
        dst[at : at + own.shape[0], offset : offset + cols, :] = jnp.where(
            row_ok, own[...].astype(F32), 0.0
        )
    sides(xf, 4, 0, tl[:, xs, :], tr[:, xs, :], has_top)
    sides(xf, 4, rows + 4, bl[:, xs, :], br[:, xs, :], has_bot)
    sides(ce, 3, 0, tl[2:4, cs, :], tr[2:4, cs, :], has_top)
    sides(ce, 3, rows + 2, bl[0:2, cs, :], br[0:2, cs, :], has_bot)

    @pl.loop(0, rows // 8)
    def _(k):
        at = pl.ds(k * 8, 8)
        sides(xf, 4, 4 + k * 8, left[at, xs, :], right[at, xs, :], None)
        sides(ce, 3, 2 + k * 8, left[at, cs, :], right[at, cs, :], None)

    per_core = n_row * nz
    n_peers = n_row + nz - 1

    def stage_all(part, pieces_of):
        stage = parts[part][0]
        for row in range(n_row):
            for col in range(n_col):
                pieces = pieces_of(row * n_col + col)
                pad = stage.shape[1] - sum(p.shape[0] for p in pieces)
                if pad:
                    pieces.append(jnp.zeros((pad, 128), F32))
                slot = (col % 2) * per_core + row * nz + col // 2
                stage[slot] = jnp.concatenate(pieces, axis=0).astype(BF16)

    def sum_copies(part, level):
        stage, recv0, acc1, recv1, acc2, recv2 = parts[part]
        if level == 0:
            todo = [(0, stage.at[pl.ds((1 - core) * per_core, per_core)], recv0)]
        elif level == 1:
            todo = [(k, acc1.at[(r + k) % n_row], recv1.at[k - 1]) for k in range(1, n_row)]
        else:
            todo = [
                (n_row - 1 + k, acc2.at[(z + k) % nz], recv2.at[k - 1]) for k in range(1, nz)
            ]
        base = 10 + part * n_peers
        return [remote(base + k, src, dst, peers[k]) for k, src, dst in todo]

    def start_sums(part, level):
        if reduce:
            for item in sum_copies(part, level):
                item.start()

    def finish_sums(part, level):
        if not reduce:
            return None
        for item in sum_copies(part, level):
            item.wait()
        stage, recv0, acc1, recv1, acc2, recv2 = parts[part]
        if level == 0:
            for k in range(per_core):
                own = stage[core * per_core + k].astype(F32)
                acc1[k // nz, k % nz] = (own + recv0[k].astype(F32)).astype(BF16)
        elif level == 1:
            for k in range(nz):
                total = acc1[r, k].astype(F32)
                for m in range(n_row - 1):
                    total = total + recv1[m, k].astype(F32)
                acc2[k] = total.astype(BF16)
        else:
            total = acc2[z].astype(F32)
            for m in range(nz - 1):
                total = total + recv2[m].astype(F32)
            return total * scale
        return None

    parts = (refs[47:53], refs[53:59])
    scale = 1.0 / math.sqrt(rows * n_row * cols * n_col)
    blocks = n_row * n_col
    nc, nd, nu = 9 * ch // blocks, 9 * ch // blocks, 4 * wide // blocks

    for at in (pl.ds(0, 4), pl.ds(rows + 4, 4)):
        shift_inputs(at, 0, 64)

    @pl.loop(0, rows // 8)
    def _(k):
        at = pl.ds(4 + k * 8, 8)
        shift_inputs(at, 0, 16)
        shift_inputs(at, 48, 16)

    wc_rows = wc[...].reshape(9 * ch, ch)
    j_at = lax.broadcasted_iota(jnp.int32, (1, 64, 1), 1) - 3
    col_ok = jnp.logical_and(
        jnp.logical_or(j_at >= 0, has_left), jnp.logical_or(j_at < cols, has_right)
    )
    def in_grid(first, n):
        i_at = lax.broadcasted_iota(jnp.int32, (n, 1, 1), 0) + (first - 3)
        row_ok = jnp.logical_and(
            jnp.logical_or(i_at >= 0, has_top), jnp.logical_or(i_at < rows, has_bot)
        )
        return jnp.logical_and(row_ok, col_ok)

    step = a_rows // 2

    @pl.loop(0, 2)
    def _(k):
        windows = [
            x3[pl.ds(k * step + p, step)].reshape(step * 64, 3 * ch) for p in range(3)
        ]
        pre = dot(jnp.concatenate(windows, axis=1), wc_rows)
        sig = jax.nn.sigmoid(pre)
        at = pl.ds(k * step, step)
        ok = in_grid(k * step, step)
        value = (pre * sig).reshape(step, 64, ch)
        fine[at, 0:64, :] = jnp.where(ok, value, 0.0)
        slope[at, 0:64, :] = (sig * (1.0 + pre * (1.0 - sig))).reshape(step, 64, ch)

    @pl.loop(0, a_rows // 2)
    def _(k):
        for p in range(2):
            for q in range(3):
                d3[k, p, :, q * ch : (q + 1) * ch] = fine[
                    2 * k + p, pl.ds(q, 32, stride=2), :
                ].astype(BF16)

    @pl.loop(0, u_rows)
    def _(k):
        for p in range(2):
            for q in range(2):
                e = 2 * p + q
                t4[k, :, e * ch : (e + 1) * ch] = ce[
                    2 * k + p, pl.ds(1 + q, 32, stride=2), :
                ].astype(BF16)

    windows = [
        d3[p // 2 : p // 2 + u_rows, p % 2].reshape(u_rows * 32, 3 * ch) for p in range(3)
    ]
    cpre = dot(jnp.concatenate(windows, axis=1), wd[...].reshape(9 * ch, wide))
    cp[...] = cpre.reshape(u_rows, 32, wide)
    v_at = lax.broadcasted_iota(jnp.int32, (1, 32, 1), 1) - 1
    v_own = jnp.logical_and(v_at >= 0, v_at < cols // 2)
    sig = jax.nn.sigmoid(cp[...])
    co[...] = (cp[...] * sig).astype(BF16)
    grad = None
    for e in range(4):
        term = dot_nt(
            t4[:, :, e * ch : (e + 1) * ch].reshape(u_rows * 32, ch), wu[e // 2, e % 2]
        )
        grad = term if grad is None else grad + term
    u_at = lax.broadcasted_iota(jnp.int32, (u_rows, 1, 1), 0) - 1
    ok = jnp.logical_and(
        jnp.logical_and(jnp.logical_or(u_at >= 0, has_top), jnp.logical_or(u_at < half, has_bot)),
        jnp.logical_and(
            jnp.logical_or(v_at >= 0, has_left), jnp.logical_or(v_at < cols // 2, has_right)
        ),
    )
    full = cp[...]
    sig = jax.nn.sigmoid(full)
    part = grad.reshape(u_rows, 32, wide) * (sig * (1.0 + full * (1.0 - sig)))
    g[:, 32:40, :] = jnp.zeros((u_rows, 8, wide), F32)
    g[:, 0:32, :] = jnp.where(ok, part, 0.0)

    own_co = jnp.where(v_own, co[1 : half + 1].astype(F32), 0.0).astype(BF16)
    us = dot_tn(own_co.reshape(half * 32, wide), t4[1 : half + 1].reshape(half * 32, 4 * ch))
    for e in range(4):
        up_sum[e * wide : (e + 1) * wide, :] = us[:, e * ch : (e + 1) * ch]
    own_g = jnp.where(v_own, g[1 : half + 1, 0:32, :], 0.0).astype(BF16).reshape(half * 32, wide)
    for p in range(3):
        window = d3[p // 2 + 1 : p // 2 + 1 + half, p % 2].reshape(half * 32, 3 * ch)
        down_sum[p * 3 * ch : (p + 1) * 3 * ch, :] = dot_tn(window, own_g)

    if reduce:
        stage_all(
            0,
            lambda d: [
                up_sum[d * nu : (d + 1) * nu, :],
                down_sum[d * nd : (d + 1) * nd, 0:128],
                down_sum[d * nd : (d + 1) * nd, 128:256],
            ],
        )
    start_sums(0, 0)

    g_here = g[:, 0:32, :].astype(BF16).reshape(u_rows * 32, wide)
    g_next = g[:, 1:33, :].astype(BF16).reshape(u_rows * 32, wide)
    less = (u_rows - 1) * 32

    def pair(p):
        return jnp.concatenate([wd[p, 1], wd[p, 2]], axis=0)

    even = dot_nt(g_here, pair(1))
    even_odd = even[:, ch:] + dot_nt(g_next, wd[1, 0])
    odd = dot_nt(g_here[32:], pair(0)) + dot_nt(g_here[:less], pair(2))
    odd_odd = odd[:, ch:] + dot_nt(g_next[32:], wd[0, 0]) + dot_nt(g_next[:less], wd[2, 0])
    spread = {
        (0, 0): even[:, :ch],
        (0, 1): even_odd,
        (1, 0): odd[:, :ch],
        (1, 1): odd_odd,
    }
    for (s, t), value in spread.items():
        for u in range(u_rows - s):
            at = pl.ds(1 + t, 32, stride=2)
            ce[2 * u + s, at, :] = ce[2 * u + s, at, :] + value[u * 32 : (u + 1) * 32]

    finish_sums(0, 0)
    start_sums(0, 1)

    @pl.loop(0, (rows + 2) // 2)
    def _(k):
        a = 2 + 2 * k
        value = ce[pl.ds(a - 1, 2), 0:64, :] * slope[pl.ds(a, 2), 0:64, :]
        gp[pl.ds(a, 2), 0:64, :] = jnp.where(in_grid(a, 2), value, 0.0)

    j_own = jnp.logical_and(j_at >= 0, j_at < cols)
    own = jnp.where(j_own, gp[3 : rows + 3, 0:64, :], 0.0).astype(BF16)

    def shift(p):
        pieces = [own]
        if p > 0:
            pieces.insert(0, jnp.zeros((p, 64, ch), BF16))
        if p < 2:
            pieces.append(jnp.zeros((2 - p, 64, ch), BF16))
        return jnp.concatenate(pieces, axis=0).reshape((rows + 2) * 64, ch)

    shifted = [shift(p) for p in range(3)]
    sums = dot_tn(
        x3[3 : rows + 5].reshape((rows + 2) * 64, 3 * ch), jnp.concatenate(shifted, axis=1)
    )
    for p in range(3):
        conv_sum[p * 3 * ch : (p + 1) * 3 * ch, :] = sums[:, p * ch : (p + 1) * ch]

    if reduce:
        stage_all(1, lambda d: [conv_sum[d * nc : (d + 1) * nc, :]])
    start_sums(1, 0)

    @pl.loop(0, (rows + 2) // 2)
    def _(k):
        at = pl.ds(2 + 2 * k, 2)
        for q in range(3):
            g3[at, :, q * ch : (q + 1) * ch] = gp[at, 4 - q : 68 - q, :].astype(BF16)

    co_rows = co[1 : half + 1].reshape(half * 32, wide)
    for e in range(4):
        p, q = e // 2, e % 2
        res = dot(co_rows, wu[p, q]).reshape(half, 32, ch)
        for m in range(half):
            up[2 * m + p, pl.ds(1 + q, 32, stride=2), :] = res[m]

    @pl.loop(0, rows // 4)
    def _(k):
        f = fine[pl.ds(3 + k * 4, 4), 3 : 3 + cols, :].astype(BF16).astype(F32)
        out_ref[pl.ds(k * 4, 4)] = (f + up[pl.ds(k * 4, 4), 3 : 3 + cols, :]).astype(BF16)

    out_copy = pltpu.make_async_copy(out_ref, out_hbm, local_sem.at[5])
    out_copy.start()
    finish_sums(1, 0)
    start_sums(1, 1)
    finish_sums(0, 1)
    start_sums(0, 2)

    turned = jnp.concatenate([wc[p, q] for p in range(3) for q in range(3)], axis=1)
    part_rows = rows // 2

    def half_inputs(k):
        windows = [
            g3[k * part_rows + 4 - p : (k + 1) * part_rows + 4 - p].reshape(
                part_rows * 64, 3 * ch
            )
            for p in range(3)
        ]
        total = dot_nt(jnp.concatenate(windows, axis=1), turned)
        total = total.reshape(part_rows, 64, ch)[:, :cols, :]
        at = pl.ds(k * part_rows, part_rows)
        gx_ref[at] = total.astype(BF16)
        done = pltpu.make_async_copy(gx_ref.at[at], gx_hbm.at[at], local_sem.at[6 + k])
        done.start()
        return done

    first_half = half_inputs(0)
    finish_sums(1, 1)
    start_sums(1, 2)
    second_half = half_inputs(1)
    total = finish_sums(0, 2)
    if reduce:
        up_out[...] = total[0:nu]
        down_out[pl.ds(0, nd, stride=2), :] = total[nu : nu + nd]
        down_out[pl.ds(1, nd, stride=2), :] = total[nu + nd : nu + 2 * nd]
    total = finish_sums(1, 2)
    if reduce:
        conv_out[...] = total[0:nc]
    for item in (out_copy, first_half, second_half):
        item.wait()


def results_kernel(n, *refs):
    given, out, held, (in_sem, out_sem) = refs[:n], refs[n : 2 * n], refs[2 * n : 3 * n], refs[3 * n :]
    pieces = []
    for k in range(n):
        size = given[k].shape[0]
        step = size // 2 if len(given[k].shape) == 3 else size
        pieces += [(k, pl.ds(at, step)) for at in range(0, size, step)]
    loads = [
        pltpu.make_async_copy(given[k].at[at], held[k].at[at], in_sem.at[m])
        for m, (k, at) in enumerate(pieces)
    ]
    stores = [
        pltpu.make_async_copy(held[k].at[at], out[k].at[at], out_sem.at[m])
        for m, (k, at) in enumerate(pieces)
    ]
    for item in loads:
        item.start()
    for load, store in zip(loads, stores):
        load.wait()
        store.start()
    for item in stores:
        item.wait()


def results(arrays):
    anywhere = pl.BlockSpec(memory_space=pl.ANY)
    n = len(arrays)
    return pl.pallas_call(
        functools.partial(results_kernel, n),
        out_shape=[jax.ShapeDtypeStruct(a.shape, a.dtype) for a in arrays],
        in_specs=[anywhere] * n,
        out_specs=[anywhere] * n,
        scratch_shapes=[pltpu.VMEM(a.shape, a.dtype) for a in arrays]
        + [pltpu.SemaphoreType.DMA((2 * n,))] * 2,
        compiler_params=pltpu.CompilerParams(vmem_limit_bytes=60 * 2**20),
        name="results",
    )(*arrays)


def body(n_row, n_col, x, ct, wc, wd, wu):
    rows, cols, ch = x.shape
    wide = wd.shape[3]
    a_rows, u_rows = rows + 6, rows // 2 + 2
    blocks, nz = n_row * n_col, n_col // 2
    sums = [(9 * ch, ch), (9 * ch, wide), (4 * wide, ch)]
    reduce = all(n % blocks == 0 for n, _ in sums)
    edges = [(4, cols, ch)] * 2 + [(2, cols, ch)] * 2 + [(rows, 16, ch)] * 2 + [(4, 16, ch)] * 4
    n_sems = 10
    scratch = [pltpu.VMEM(a.shape, BF16) for a in (x, ct, wc, wd, wu, x, x)]
    scratch += [pltpu.VMEM((2, rows, 16, ch), BF16)]
    scratch += [pltpu.VMEM(e, BF16) for e in edges]
    scratch += [
        pltpu.VMEM((rows + 8, 72, ch), F32),
        pltpu.VMEM((rows + 8, 64, 3 * ch), BF16),
        pltpu.VMEM((rows + 4, 72, ch), F32),
        pltpu.VMEM((a_rows, 72, ch), F32),
        pltpu.VMEM((a_rows, 72, ch), F32),
        pltpu.VMEM((a_rows // 2, 2, 32, 3 * ch), BF16),
        pltpu.VMEM((u_rows, 32, 4 * ch), BF16),
        pltpu.VMEM((u_rows, 32, wide), F32),
        pltpu.VMEM((u_rows, 32, wide), BF16),
        pltpu.VMEM((u_rows, 40, wide), F32),
        pltpu.VMEM((a_rows, 72, ch), F32),
        pltpu.VMEM((a_rows, 64, 3 * ch), BF16),
        pltpu.VMEM((rows, 72, ch), F32),
    ]
    more = []
    if reduce:
        n_sems += 2 * (n_row + nz - 1)
        more += [pltpu.VMEM(s, F32) for s in sums]
        heights = (sums[2][0] + 2 * sums[1][0]) // blocks, sums[0][0] // blocks
        for height in heights:
            height = -(-height // 16) * 16
            for lead in (
                (blocks,), (blocks // 2,), (n_row, nz), (n_row - 1, nz), (nz,), (nz - 1,)
            ):
                more.append(pltpu.VMEM(lead + (height, 128), BF16))
        outs = [(n * w // blocks // 128, 128) for n, w in sums]
    else:
        outs = sums
    scratch += [pltpu.SemaphoreType.DMA((n_sems,))] * 2 + [pltpu.SemaphoreType.DMA((8,))] + more
    anywhere = pl.BlockSpec(memory_space=pl.ANY)
    found = pl.pallas_call(
        functools.partial(level_kernel, n_row, n_col, reduce),
        out_shape=[jax.ShapeDtypeStruct(x.shape, BF16)] * 2
        + [jax.ShapeDtypeStruct(s, F32) for s in outs],
        in_specs=[anywhere] * 5,
        out_specs=[anywhere] * 2 + [VMEM] * 3,
        scratch_shapes=scratch,
        compiler_params=pltpu.CompilerParams(
            collective_id=0, has_side_effects=True, vmem_limit_bytes=60 * 2**20
        ),
        name="level",
    )(x, ct, wc, wd, wu)
    output, grad_inputs, *sums = results(found)
    sums = [a.reshape(-1) for a in sums]
    if not reduce:
        scale = 1.0 / math.sqrt(rows * n_row * cols * n_col)
        sums = [
            lax.psum_scatter(a, ("row", "col"), scatter_dimension=0, tiled=True) * scale
            for a in sums
        ]
    return (output, grad_inputs, *sums)


def solution(mesh):
    return jax.shard_map(
        functools.partial(body, mesh.shape["row"], mesh.shape["col"]),
        mesh=mesh,
        in_specs=(P("row", "col", None), P("row", "col", None), P(), P(), P()),
        out_specs=(
            P("row", "col", None),
            P("row", "col", None),
            P(("row", "col")),
            P(("row", "col")),
            P(("row", "col")),
        ),
        check_vma=False,
    )
```

```python
import functools
import math

import jax
import jax.numpy as jnp
from jax import lax
from jax.experimental import pallas as pl
from jax.experimental.pallas import tpu as pltpu
from jax.sharding import PartitionSpec as P

MESH = pl.DeviceIdType.MESH
F32 = jnp.float32
BF16 = jnp.bfloat16
VMEM = pl.BlockSpec(memory_space=pltpu.VMEM)
NT = (((1,), (1,)), ((), ()))
TN = (((0,), (0,)), ((), ()))
SHIFTS = [(dr, dc) for dr in (-1, 0, 1) for dc in (-1, 0, 1) if (dr, dc) != (0, 0)]


def dot(a, b):
    return jnp.dot(a, b, preferred_element_type=F32)


def dot_nt(a, b):
    return lax.dot_general(a, b, NT, preferred_element_type=F32)


def dot_tn(a, b):
    return lax.dot_general(a, b, TN, preferred_element_type=F32)


def exists(at, n, d):
    return at > 0 if d < 0 else at < n - 1


def level_kernel(n_row, n_col, reduce, *refs):
    x_hbm, ct_hbm, wc_hbm, wd_hbm, wu_hbm, out_hbm, gx_hbm, conv_out, down_out, up_out = refs[:10]
    x_ref, ct_ref, wc, wd, wu, out_ref, gx_ref, pack = refs[10:18]
    x_top, x_bot, ct_top, ct_bot, left, right, tl, tr, bl, br = edges = refs[18:28]
    (xf, x3, ce, fine, slope, d3, t4, cp, co, g, gp, g3, up) = refs[28:41]
    send_sem, recv_sem, local_sem = refs[41:44]
    conv_sum, down_sum, up_sum = refs[44:47] if reduce else (conv_out, down_out, up_out)
    rows, cols, ch = x_ref.shape
    wide = wd.shape[3]
    nz = n_col // 2
    r, c = lax.axis_index("row"), lax.axis_index("col")
    z, core = c // 2, c % 2
    has_top, has_bot = r > 0, r < n_row - 1
    has_left, has_right = c > 0, c < n_col - 1
    ce_rows, a_rows, u_rows = rows + 4, rows + 6, rows // 2 + 2
    half = rows // 2

    loads = [
        pltpu.make_async_copy(src, dst, local_sem.at[k])
        for k, (src, dst) in enumerate(
            [(x_hbm, x_ref), (ct_hbm, ct_ref), (wc_hbm, wc), (wd_hbm, wd), (wu_hbm, wu)]
        )
    ]

    def near(dr, dc):
        ok = None
        for d, at, n in ((dr, r, n_row), (dc, c, n_col)):
            if d:
                here = exists(at, n, d)
                ok = here if ok is None else jnp.logical_and(ok, here)
        return ok

    peers = [(r, z * 2 + 1 - core)]
    peers += [((r + k) % n_row, c) for k in range(1, n_row)]
    peers += [(r, ((z + k) % nz) * 2 + core) for k in range(1, nz)]
    if not reduce:
        peers = []
    barrier = pltpu.get_barrier_semaphore()
    for dr, dc in SHIFTS:

        @pl.when(near(dr, dc))
        def _(dr=dr, dc=dc):
            pl.semaphore_signal(barrier, inc=1, device_id=(r + dr, c + dc), device_id_type=MESH)

    for peer in peers:
        pl.semaphore_signal(barrier, inc=1, device_id=peer, device_id_type=MESH)

    for item in loads:
        item.start()

    loads[0].wait()
    loads[1].wait()
    for side, at in ((0, 0), (1, cols - 8)):
        pack[side] = jnp.concatenate(
            [x_ref[:, at : at + 8, :].astype(F32), ct_ref[:, at : at + 8, :].astype(F32)], axis=1
        ).astype(BF16)
    near_r = 3 - (r == 0).astype(jnp.int32) - (r == n_row - 1).astype(jnp.int32)
    near_c = 3 - (c == 0).astype(jnp.int32) - (c == n_col - 1).astype(jnp.int32)
    pl.semaphore_wait(barrier, near_r * near_c - 1 + len(peers))

    low, high = pl.ds(0, 4), pl.ds(rows - 4, 4)
    plan = [
        ((1, 0), x_ref.at[high], x_top),
        ((-1, 0), x_ref.at[low], x_bot),
        ((1, 0), ct_ref.at[pl.ds(rows - 2, 2)], ct_top),
        ((-1, 0), ct_ref.at[pl.ds(0, 2)], ct_bot),
        ((0, 1), pack.at[1], left),
        ((0, -1), pack.at[0], right),
        ((1, 1), pack.at[1, high], tl),
        ((1, -1), pack.at[0, high], tr),
        ((-1, 1), pack.at[1, low], bl),
        ((-1, -1), pack.at[0, low], br),
    ]

    def remote(k, src, dst, device):
        return pltpu.make_async_remote_copy(
            src_ref=src,
            dst_ref=dst,
            send_sem=send_sem.at[k],
            recv_sem=recv_sem.at[k],
            device_id=device,
            device_id_type=MESH,
        )

    def edge(k):
        (dr, dc), src, dst = plan[k]
        return remote(k, src, dst, (r + dr, c + dc))

    for k, ((dr, dc), _, _) in enumerate(plan):

        @pl.when(near(dr, dc))
        def _(k=k):
            edge(k).start()

    xf[:, 64:72, :] = jnp.zeros((rows + 8, 8, ch), F32)
    ce[:, 64:72, :] = jnp.zeros((ce_rows, 8, ch), F32)
    fine[:, 64:72, :] = jnp.zeros((a_rows, 8, ch), F32)
    slope[:, 64:72, :] = jnp.zeros((a_rows, 8, ch), F32)
    gp[:, 64:72, :] = jnp.zeros((a_rows, 8, ch), F32)

    def shift_inputs(at, first, n):
        for q in range(3):
            x3[at, first : first + n, q * ch : (q + 1) * ch] = xf[
                at, first + q : first + q + n, :
            ].astype(BF16)

    xf[:, 0:8, :] = jnp.zeros((rows + 8, 8, ch), F32)
    xf[:, 56:64, :] = jnp.zeros((rows + 8, 8, ch), F32)

    @pl.loop(0, rows // 4)
    def _(k):
        at = pl.ds(k * 4, 4)
        xf[pl.ds(4 + k * 4, 4), 4 : 4 + cols, :] = x_ref[at].astype(F32)
        ce[pl.ds(2 + k * 4, 4), 3 : 3 + cols, :] = ct_ref[at].astype(F32)
        shift_inputs(pl.ds(4 + k * 4, 4), 16, 32)

    for item in loads[2:]:
        item.wait()
    for k, ((dr, dc), _, _) in enumerate(plan):

        @pl.when(near(dr, dc))
        def _(k=k):
            edge(k).wait_send()

        @pl.when(near(-dr, -dc))
        def _(k=k):
            edge(k).wait_recv()

    def sides(dst, offset, at, lft, rgt, row_ok):
        ok_l, ok_r = has_left, has_right
        if row_ok is not None:
            ok_l = jnp.logical_and(ok_l, row_ok)
            ok_r = jnp.logical_and(ok_r, row_ok)
        rows_at = pl.ds(at, lft.shape[0])
        dst[rows_at, 0:offset, :] = jnp.where(ok_l, lft.astype(F32), 0.0)[:, 8 - offset : 8, :]
        dst[rows_at, offset + cols : offset + cols + 8, :] = jnp.where(ok_r, rgt.astype(F32), 0.0)

    xs, cs = slice(0, 8), slice(8, 16)
    for dst, offset, at, own, row_ok in (
        (xf, 4, 0, x_top, has_top),
        (xf, 4, rows + 4, x_bot, has_bot),
        (ce, 3, 0, ct_top, has_top),
        (ce, 3, rows + 2, ct_bot, has_bot),
    ):
        dst[at : at + own.shape[0], offset : offset + cols, :] = jnp.where(
            row_ok, own[...].astype(F32), 0.0
        )
    sides(xf, 4, 0, tl[:, xs, :], tr[:, xs, :], has_top)
    sides(xf, 4, rows + 4, bl[:, xs, :], br[:, xs, :], has_bot)
    sides(ce, 3, 0, tl[2:4, cs, :], tr[2:4, cs, :], has_top)
    sides(ce, 3, rows + 2, bl[0:2, cs, :], br[0:2, cs, :], has_bot)

    @pl.loop(0, rows // 8)
    def _(k):
        at = pl.ds(k * 8, 8)
        sides(xf, 4, 4 + k * 8, left[at, xs, :], right[at, xs, :], None)
        sides(ce, 3, 2 + k * 8, left[at, cs, :], right[at, cs, :], None)

    per_core = n_row * nz
    n_peers = n_row + nz - 1

    def stage_all(part, pieces_of):
        stage = parts[part][0]
        for row in range(n_row):
            for col in range(n_col):
                pieces = pieces_of(row * n_col + col)
                pad = stage.shape[1] - sum(p.shape[0] for p in pieces)
                if pad:
                    pieces.append(jnp.zeros((pad, 128), F32))
                slot = (col % 2) * per_core + row * nz + col // 2
                stage[slot] = jnp.concatenate(pieces, axis=0).astype(BF16)

    def sum_copies(part, level):
        stage, recv0, acc1, recv1, acc2, recv2 = parts[part]
        if level == 0:
            todo = [(0, stage.at[pl.ds((1 - core) * per_core, per_core)], recv0)]
        elif level == 1:
            todo = [(k, acc1.at[(r + k) % n_row], recv1.at[k - 1]) for k in range(1, n_row)]
        else:
            todo = [
                (n_row - 1 + k, acc2.at[(z + k) % nz], recv2.at[k - 1]) for k in range(1, nz)
            ]
        base = 10 + part * n_peers
        return [remote(base + k, src, dst, peers[k]) for k, src, dst in todo]

    def start_sums(part, level):
        if reduce:
            for item in sum_copies(part, level):
                item.start()

    def finish_sums(part, level):
        if not reduce:
            return None
        for item in sum_copies(part, level):
            item.wait()
        stage, recv0, acc1, recv1, acc2, recv2 = parts[part]
        if level == 0:
            for k in range(per_core):
                own = stage[core * per_core + k].astype(F32)
                acc1[k // nz, k % nz] = (own + recv0[k].astype(F32)).astype(BF16)
        elif level == 1:
            for k in range(nz):
                total = acc1[r, k].astype(F32)
                for m in range(n_row - 1):
                    total = total + recv1[m, k].astype(F32)
                acc2[k] = total.astype(BF16)
        else:
            total = acc2[z].astype(F32)
            for m in range(nz - 1):
                total = total + recv2[m].astype(F32)
            return total * scale
        return None

    parts = (refs[47:53], refs[53:59])
    scale = 1.0 / math.sqrt(rows * n_row * cols * n_col)
    blocks = n_row * n_col
    nc, nd, nu = 9 * ch // blocks, 9 * ch // blocks, 4 * wide // blocks

    for at in (pl.ds(0, 4), pl.ds(rows + 4, 4)):
        shift_inputs(at, 0, 64)

    @pl.loop(0, rows // 8)
    def _(k):
        at = pl.ds(4 + k * 8, 8)
        shift_inputs(at, 0, 16)
        shift_inputs(at, 48, 16)

    wc_rows = wc[...].reshape(9 * ch, ch)
    j_at = lax.broadcasted_iota(jnp.int32, (1, 64, 1), 1) - 3
    col_ok = jnp.logical_and(
        jnp.logical_or(j_at >= 0, has_left), jnp.logical_or(j_at < cols, has_right)
    )
    def in_grid(first, n):
        i_at = lax.broadcasted_iota(jnp.int32, (n, 1, 1), 0) + (first - 3)
        row_ok = jnp.logical_and(
            jnp.logical_or(i_at >= 0, has_top), jnp.logical_or(i_at < rows, has_bot)
        )
        return jnp.logical_and(row_ok, col_ok)

    step = a_rows // 2

    @pl.loop(0, 2)
    def _(k):
        windows = [
            x3[pl.ds(k * step + p, step)].reshape(step * 64, 3 * ch) for p in range(3)
        ]
        pre = dot(jnp.concatenate(windows, axis=1), wc_rows)
        sig = jax.nn.sigmoid(pre)
        at = pl.ds(k * step, step)
        ok = in_grid(k * step, step)
        value = (pre * sig).reshape(step, 64, ch)
        fine[at, 0:64, :] = jnp.where(ok, value, 0.0)
        slope[at, 0:64, :] = (sig * (1.0 + pre * (1.0 - sig))).reshape(step, 64, ch)

    @pl.loop(0, a_rows // 2)
    def _(k):
        for p in range(2):
            for q in range(3):
                d3[k, p, :, q * ch : (q + 1) * ch] = fine[
                    2 * k + p, pl.ds(q, 32, stride=2), :
                ].astype(BF16)

    @pl.loop(0, u_rows)
    def _(k):
        for p in range(2):
            for q in range(2):
                e = 2 * p + q
                t4[k, :, e * ch : (e + 1) * ch] = ce[
                    2 * k + p, pl.ds(1 + q, 32, stride=2), :
                ].astype(BF16)

    windows = [
        d3[p // 2 : p // 2 + u_rows, p % 2].reshape(u_rows * 32, 3 * ch) for p in range(3)
    ]
    cpre = dot(jnp.concatenate(windows, axis=1), wd[...].reshape(9 * ch, wide))
    cp[...] = cpre.reshape(u_rows, 32, wide)
    v_at = lax.broadcasted_iota(jnp.int32, (1, 32, 1), 1) - 1
    v_own = jnp.logical_and(v_at >= 0, v_at < cols // 2)
    sig = jax.nn.sigmoid(cp[...])
    co[...] = (cp[...] * sig).astype(BF16)
    grad = None
    for e in range(4):
        term = dot_nt(
            t4[:, :, e * ch : (e + 1) * ch].reshape(u_rows * 32, ch), wu[e // 2, e % 2]
        )
        grad = term if grad is None else grad + term
    u_at = lax.broadcasted_iota(jnp.int32, (u_rows, 1, 1), 0) - 1
    ok = jnp.logical_and(
        jnp.logical_and(jnp.logical_or(u_at >= 0, has_top), jnp.logical_or(u_at < half, has_bot)),
        jnp.logical_and(
            jnp.logical_or(v_at >= 0, has_left), jnp.logical_or(v_at < cols // 2, has_right)
        ),
    )
    full = cp[...]
    sig = jax.nn.sigmoid(full)
    part = grad.reshape(u_rows, 32, wide) * (sig * (1.0 + full * (1.0 - sig)))
    g[:, 32:40, :] = jnp.zeros((u_rows, 8, wide), F32)
    g[:, 0:32, :] = jnp.where(ok, part, 0.0)

    own_co = jnp.where(v_own, co[1 : half + 1].astype(F32), 0.0).astype(BF16)
    us = dot_tn(own_co.reshape(half * 32, wide), t4[1 : half + 1].reshape(half * 32, 4 * ch))
    for e in range(4):
        up_sum[e * wide : (e + 1) * wide, :] = us[:, e * ch : (e + 1) * ch]
    own_g = jnp.where(v_own, g[1 : half + 1, 0:32, :], 0.0).astype(BF16).reshape(half * 32, wide)
    for p in range(3):
        window = d3[p // 2 + 1 : p // 2 + 1 + half, p % 2].reshape(half * 32, 3 * ch)
        down_sum[p * 3 * ch : (p + 1) * 3 * ch, :] = dot_tn(window, own_g)

    if reduce:
        stage_all(
            0,
            lambda d: [
                up_sum[d * nu : (d + 1) * nu, :],
                down_sum[d * nd : (d + 1) * nd, 0:128],
                down_sum[d * nd : (d + 1) * nd, 128:256],
            ],
        )
    start_sums(0, 0)

    g_here = g[:, 0:32, :].astype(BF16).reshape(u_rows * 32, wide)
    g_next = g[:, 1:33, :].astype(BF16).reshape(u_rows * 32, wide)
    less = (u_rows - 1) * 32

    def pair(p):
        return jnp.concatenate([wd[p, 1], wd[p, 2]], axis=0)

    even = dot_nt(g_here, pair(1))
    even_odd = even[:, ch:] + dot_nt(g_next, wd[1, 0])
    odd = dot_nt(g_here[32:], pair(0)) + dot_nt(g_here[:less], pair(2))
    odd_odd = odd[:, ch:] + dot_nt(g_next[32:], wd[0, 0]) + dot_nt(g_next[:less], wd[2, 0])
    spread = {
        (0, 0): even[:, :ch],
        (0, 1): even_odd,
        (1, 0): odd[:, :ch],
        (1, 1): odd_odd,
    }
    for (s, t), value in spread.items():
        for u in range(u_rows - s):
            at = pl.ds(1 + t, 32, stride=2)
            ce[2 * u + s, at, :] = ce[2 * u + s, at, :] + value[u * 32 : (u + 1) * 32]

    finish_sums(0, 0)
    start_sums(0, 1)

    @pl.loop(0, (rows + 2) // 2)
    def _(k):
        a = 2 + 2 * k
        value = ce[pl.ds(a - 1, 2), 0:64, :] * slope[pl.ds(a, 2), 0:64, :]
        gp[pl.ds(a, 2), 0:64, :] = jnp.where(in_grid(a, 2), value, 0.0)

    j_own = jnp.logical_and(j_at >= 0, j_at < cols)
    own = jnp.where(j_own, gp[3 : rows + 3, 0:64, :], 0.0).astype(BF16)

    def shift(p):
        pieces = [own]
        if p > 0:
            pieces.insert(0, jnp.zeros((p, 64, ch), BF16))
        if p < 2:
            pieces.append(jnp.zeros((2 - p, 64, ch), BF16))
        return jnp.concatenate(pieces, axis=0).reshape((rows + 2) * 64, ch)

    shifted = [shift(p) for p in range(3)]
    sums = dot_tn(
        x3[3 : rows + 5].reshape((rows + 2) * 64, 3 * ch), jnp.concatenate(shifted, axis=1)
    )
    for p in range(3):
        conv_sum[p * 3 * ch : (p + 1) * 3 * ch, :] = sums[:, p * ch : (p + 1) * ch]

    if reduce:
        stage_all(1, lambda d: [conv_sum[d * nc : (d + 1) * nc, :]])
    start_sums(1, 0)

    @pl.loop(0, (rows + 2) // 2)
    def _(k):
        at = pl.ds(2 + 2 * k, 2)
        for q in range(3):
            g3[at, :, q * ch : (q + 1) * ch] = gp[at, 4 - q : 68 - q, :].astype(BF16)

    finish_sums(1, 0)
    start_sums(1, 1)
    finish_sums(0, 1)
    start_sums(0, 2)

    co_rows = co[1 : half + 1].reshape(half * 32, wide)
    for e in range(4):
        p, q = e // 2, e % 2
        res = dot(co_rows, wu[p, q]).reshape(half, 32, ch)
        for m in range(half):
            up[2 * m + p, pl.ds(1 + q, 32, stride=2), :] = res[m]

    @pl.loop(0, rows // 4)
    def _(k):
        f = fine[pl.ds(3 + k * 4, 4), 3 : 3 + cols, :].astype(BF16).astype(F32)
        out_ref[pl.ds(k * 4, 4)] = (f + up[pl.ds(k * 4, 4), 3 : 3 + cols, :]).astype(BF16)

    out_copy = pltpu.make_async_copy(out_ref, out_hbm, local_sem.at[5])
    out_copy.start()
    turned = jnp.concatenate([wc[p, q] for p in range(3) for q in range(3)], axis=1)
    part_rows = rows // 2

    def half_inputs(k):
        windows = [
            g3[k * part_rows + 4 - p : (k + 1) * part_rows + 4 - p].reshape(
                part_rows * 64, 3 * ch
            )
            for p in range(3)
        ]
        total = dot_nt(jnp.concatenate(windows, axis=1), turned)
        total = total.reshape(part_rows, 64, ch)[:, :cols, :]
        at = pl.ds(k * part_rows, part_rows)
        gx_ref[at] = total.astype(BF16)
        done = pltpu.make_async_copy(gx_ref.at[at], gx_hbm.at[at], local_sem.at[6 + k])
        done.start()
        return done

    first_half = half_inputs(0)
    finish_sums(1, 1)
    start_sums(1, 2)
    second_half = half_inputs(1)
    total = finish_sums(0, 2)
    if reduce:
        up_out[...] = total[0:nu]
        down_out[pl.ds(0, nd, stride=2), :] = total[nu : nu + nd]
        down_out[pl.ds(1, nd, stride=2), :] = total[nu + nd : nu + 2 * nd]
    total = finish_sums(1, 2)
    if reduce:
        conv_out[...] = total[0:nc]
    for item in (out_copy, first_half, second_half):
        item.wait()


def results_kernel(n, *refs):
    given, out, held, (in_sem, out_sem) = refs[:n], refs[n : 2 * n], refs[2 * n : 3 * n], refs[3 * n :]
    pieces = []
    for k in range(n):
        size = given[k].shape[0]
        step = size // 2 if len(given[k].shape) == 3 else size
        pieces += [(k, pl.ds(at, step)) for at in range(0, size, step)]
    loads = [
        pltpu.make_async_copy(given[k].at[at], held[k].at[at], in_sem.at[m])
        for m, (k, at) in enumerate(pieces)
    ]
    stores = [
        pltpu.make_async_copy(held[k].at[at], out[k].at[at], out_sem.at[m])
        for m, (k, at) in enumerate(pieces)
    ]
    for item in loads:
        item.start()
    for load, store in zip(loads, stores):
        load.wait()
        store.start()
    for item in stores:
        item.wait()


def results(arrays):
    anywhere = pl.BlockSpec(memory_space=pl.ANY)
    n = len(arrays)
    return pl.pallas_call(
        functools.partial(results_kernel, n),
        out_shape=[jax.ShapeDtypeStruct(a.shape, a.dtype) for a in arrays],
        in_specs=[anywhere] * n,
        out_specs=[anywhere] * n,
        scratch_shapes=[pltpu.VMEM(a.shape, a.dtype) for a in arrays]
        + [pltpu.SemaphoreType.DMA((2 * n,))] * 2,
        compiler_params=pltpu.CompilerParams(vmem_limit_bytes=60 * 2**20),
        name="results",
    )(*arrays)


def body(n_row, n_col, x, ct, wc, wd, wu):
    rows, cols, ch = x.shape
    wide = wd.shape[3]
    a_rows, u_rows = rows + 6, rows // 2 + 2
    blocks, nz = n_row * n_col, n_col // 2
    sums = [(9 * ch, ch), (9 * ch, wide), (4 * wide, ch)]
    reduce = all(n % blocks == 0 for n, _ in sums)
    edges = [(4, cols, ch)] * 2 + [(2, cols, ch)] * 2 + [(rows, 16, ch)] * 2 + [(4, 16, ch)] * 4
    n_sems = 10
    scratch = [pltpu.VMEM(a.shape, BF16) for a in (x, ct, wc, wd, wu, x, x)]
    scratch += [pltpu.VMEM((2, rows, 16, ch), BF16)]
    scratch += [pltpu.VMEM(e, BF16) for e in edges]
    scratch += [
        pltpu.VMEM((rows + 8, 72, ch), F32),
        pltpu.VMEM((rows + 8, 64, 3 * ch), BF16),
        pltpu.VMEM((rows + 4, 72, ch), F32),
        pltpu.VMEM((a_rows, 72, ch), F32),
        pltpu.VMEM((a_rows, 72, ch), F32),
        pltpu.VMEM((a_rows // 2, 2, 32, 3 * ch), BF16),
        pltpu.VMEM((u_rows, 32, 4 * ch), BF16),
        pltpu.VMEM((u_rows, 32, wide), F32),
        pltpu.VMEM((u_rows, 32, wide), BF16),
        pltpu.VMEM((u_rows, 40, wide), F32),
        pltpu.VMEM((a_rows, 72, ch), F32),
        pltpu.VMEM((a_rows, 64, 3 * ch), BF16),
        pltpu.VMEM((rows, 72, ch), F32),
    ]
    more = []
    if reduce:
        n_sems += 2 * (n_row + nz - 1)
        more += [pltpu.VMEM(s, F32) for s in sums]
        heights = (sums[2][0] + 2 * sums[1][0]) // blocks, sums[0][0] // blocks
        for height in heights:
            height = -(-height // 16) * 16
            for lead in (
                (blocks,), (blocks // 2,), (n_row, nz), (n_row - 1, nz), (nz,), (nz - 1,)
            ):
                more.append(pltpu.VMEM(lead + (height, 128), BF16))
        outs = [(n * w // blocks // 128, 128) for n, w in sums]
    else:
        outs = sums
    scratch += [pltpu.SemaphoreType.DMA((n_sems,))] * 2 + [pltpu.SemaphoreType.DMA((8,))] + more
    anywhere = pl.BlockSpec(memory_space=pl.ANY)
    found = pl.pallas_call(
        functools.partial(level_kernel, n_row, n_col, reduce),
        out_shape=[jax.ShapeDtypeStruct(x.shape, BF16)] * 2
        + [jax.ShapeDtypeStruct(s, F32) for s in outs],
        in_specs=[anywhere] * 5,
        out_specs=[anywhere] * 2 + [VMEM] * 3,
        scratch_shapes=scratch,
        compiler_params=pltpu.CompilerParams(
            collective_id=0, has_side_effects=True, vmem_limit_bytes=60 * 2**20
        ),
        name="level",
    )(x, ct, wc, wd, wu)
    output, grad_inputs, *sums = results(found)
    sums = [a.reshape(-1) for a in sums]
    if not reduce:
        scale = 1.0 / math.sqrt(rows * n_row * cols * n_col)
        sums = [
            lax.psum_scatter(a, ("row", "col"), scatter_dimension=0, tiled=True) * scale
            for a in sums
        ]
    return (output, grad_inputs, *sums)


def solution(mesh):
    return jax.shard_map(
        functools.partial(body, mesh.shape["row"], mesh.shape["col"]),
        mesh=mesh,
        in_specs=(P("row", "col", None), P("row", "col", None), P(), P(), P()),
        out_specs=(
            P("row", "col", None),
            P("row", "col", None),
            P(("row", "col")),
            P(("row", "col")),
            P(("row", "col")),
        ),
        check_vma=False,
    )
```
